32 devices in a mesh: dp: 8 (over y, x, core), hid: 4 (over z).
Axes of the slice: x: 2, y: 2, z: 4, core: 2. Of those that a mesh axis runs over, the one named last changes fastest.
Arguments:
- tokens: bfloat16 [192, 196, 384], P('dp'), may hold values from -6 to 6
- masks: int32 [192, 196], P('dp'), may hold values 0 or 1
- cotangent: bfloat16 [192, 196, 384], P('dp'), may hold values from -6 to 6
- aff_scale: float32 [2, 2, 384], replicated, may hold values from 0.25 to 1.75
- aff_shift: float32 [2, 2, 384], replicated, may hold values from -3 to 3
- layer_scale: float32 [2, 2, 384], replicated, may hold values from 0.25 to 1.75
- crosspatch_weight: bfloat16 [2, 196, 196], replicated, may hold values from -0.4375 to 0.4375
- cross_bias: float32 [2, 196], replicated, may hold values from -3 to 3
- fc1_weight: bfloat16 [2, 384, 1536], P(None, 'dp', 'hid'), may hold values from -0.3125 to 0.3125
- fc1_bias: float32 [2, 1536], replicated, may hold values from -3 to 3
- fc2_weight: bfloat16 [2, 384, 1536], P(None, 'dp', 'hid'), may hold values from -0.15625 to 0.15625
- fc2_bias: float32 [2, 384], replicated, may hold values from -2 to 2
Outputs:
- output: bfloat16 [192, 196, 384], P('dp')
- tokens_grad: bfloat16 [192, 196, 384], P('dp')
- aff_scale_grad: float32 [2, 2, 384], replicated
- aff_shift_grad: float32 [2, 2, 384], replicated
- layer_scale_grad: float32 [2, 2, 384], replicated
- cross_weight_grad: float32 [2, 196, 196], replicated
- cross_bias_grad: float32 [2, 196], replicated
- fc1_weight_grad: float32 [2, 384, 1536], P(None, 'dp', 'hid')
- fc1_bias_grad: float32 [2, 1536], P(None, 'hid')
- fc2_weight_grad: float32 [2, 384, 1536], P(None, 'dp', 'hid')
- fc2_bias_grad: float32 [2, 384], replicated
The draws below stay inside these ranges and needn't reach their ends.
All inputs are finite; a program needn't handle non-finite values. No bound on the sum of `masks` on one device may be relied on, other than what follows from the above.
Results may differ from the reference program's by a relative error of at most 0.02.
Values may be sent and summed in bfloat16 or wider, within the bound.
No kernel may reach another device: no remote copies, remote signals or barrier semaphores. Data moves between devices by JAX's collectives and lax.ppermute only.
A program may use at most 256 MiB of HBM per device.

```python
import jax
import jax.numpy as jnp
from jax import lax

D = 384
FF = 1536
PATCHES = 196
LAYERS = 2
IMG_DEV = 24
IMAGES = 192
N_HID = 4


def with_ends(values, rng, smallest, top_value):
    place = [jax.random.randint(jax.random.fold_in(rng, axis), (), 0, length) for axis, length in enumerate(values.shape)]
    main_axis = values.shape.index(max(values.shape))
    next_to = place[:main_axis] + [(place[main_axis] + 1) % values.shape[main_axis]] + place[main_axis + 1:]
    return values.at[tuple(place)].set(smallest).at[tuple(next_to)].set(top_value)


def spiked(values, own_key, source, target, blocks, factor):
    owner, partner = [(jnp.arange(values.shape[axis_at]) // (values.shape[axis_at] // blocks)).reshape([-1 if axis == axis_at else 1 for axis in range(values.ndim)]) for axis_at in (source, target)]
    chosen = jax.random.permutation(own_key, blocks)[partner]
    strong = (owner == chosen) | (owner == (partner + blocks // 2) % blocks)
    return jnp.where(strong, factor * values, values)


def levels(rng, extent, pieces, least, top_value):
    def one(axis_at, blocks):
        heights = jax.random.uniform(jax.random.fold_in(jax.random.fold_in(rng, 6), axis_at), (blocks,), jnp.float32, least / len(pieces), top_value / len(pieces))
        return jnp.repeat(jnp.exp(heights), extent[axis_at] // blocks).reshape((-1,) + (1,) * (len(extent) - axis_at - 1))

    factor_of = one(*pieces[0])
    for cut in pieces[1:]:
        factor_of = factor_of * one(*cut)
    return factor_of


def gaussian(key, dims, width, most, split=(), dtype=jnp.bfloat16):
    drawn = width * jax.random.normal(key, dims, jnp.float32)
    if split:
        drawn = drawn * levels(key, dims, split, -0.22, 0.18)
    return jnp.clip(drawn, -most, most).astype(dtype)


def heavy_noise(rng, dims, deviation, reach, split, heavy, kind=jnp.bfloat16):
    values = deviation * jax.random.normal(rng, dims, jnp.float32)
    if split:
        values = values * levels(rng, dims, split, -0.22, 0.18)
    return jnp.clip(spiked(values, jax.random.fold_in(rng, 3), *heavy), -reach, reach).astype(kind)


def setup_inputs(seed: int = 0) -> dict:
    streams_of = jax.random.split(jax.random.key(seed), 13)
    return {
        "tokens": heavy_noise(streams_of[0], (IMAGES, PATCHES, D), 1.0, 6.0, ((0, 8),), (0, 2, 8, 2.0)),
        "masks": with_ends((jax.random.randint(streams_of[1], (IMAGES, PATCHES), 0, 4) < 3).astype(jnp.int32), jax.random.fold_in(streams_of[1], 1), 0, 1),
        "cotangent": heavy_noise(streams_of[2], (IMAGES, PATCHES, D), 1.0, 6.0, ((0, 8),), (0, 2, 8, 2.0)),
        "aff_scale": jnp.clip(1.0 + 0.15 * jax.random.normal(streams_of[3], (LAYERS, 2, D), jnp.float32), 0.25, 1.75),
        "aff_shift": gaussian(streams_of[4], (LAYERS, 2, D), 0.5, 3.0, (), jnp.float32),
        "layer_scale": jnp.clip(1.0 + 0.15 * jax.random.normal(streams_of[5], (LAYERS, 2, D), jnp.float32), 0.25, 1.75),
        "crosspatch_weight": gaussian(streams_of[6], (LAYERS, PATCHES, PATCHES), PATCHES ** -0.5, 0.4375),
        "cross_bias": gaussian(streams_of[7], (LAYERS, PATCHES), 0.5, 3.0, (), jnp.float32),
        "fc1_weight": gaussian(streams_of[8], (LAYERS, D, FF), D ** -0.5, 0.3125, ((1, 8), (2, 4))),
        "fc1_bias": gaussian(streams_of[9], (LAYERS, FF), 0.5, 3.0, (), jnp.float32),
        "fc2_weight": gaussian(streams_of[10], (LAYERS, D, FF), FF ** -0.5, 0.15625, ((1, 8), (2, 4))),
        "fc2_bias": gaussian(streams_of[11], (LAYERS, D), 0.3, 2.0, (), jnp.float32),
    }


@jax.custom_vjp
def low(v):
    return lax.optimization_barrier(v.astype(jnp.bfloat16)).astype(jnp.float32)

@jax.custom_vjp
def low_back(v):
    return v

def low_keep(v):
    return (low(v), None)

def low_pass(kept, grad):
    return (grad,)

def back_keep(v):
    return (v, None)

def back_low(kept, grad):
    return (low(grad),)
low.defvjp(low_keep, low_pass)
low_back.defvjp(back_keep, back_low)
FULL_ACCURACY = lax.Precision.HIGHEST

def gelu_exact(values):
    return jax.nn.gelu(values, approximate=False)

def layer_stack(params, stream, keep_rows):
    aff_scale, aff_shift, layer_scale, crosspatch_weight, cross_bias, fc1_weight, fc1_bias, fc2_weight, fc2_bias = params
    group_width = FF // N_HID
    for current_layer_index in range(LAYERS):
        mixed_input = low((aff_scale[current_layer_index, 0] * stream + aff_shift[current_layer_index, 0]) * keep_rows)
        patch_mixed = jnp.einsum('xu,fuo->fxo', crosspatch_weight[current_layer_index], mixed_input, precision=FULL_ACCURACY)
        patch_mixed = patch_mixed + cross_bias[current_layer_index][None, :, None]
        middle = stream + layer_scale[current_layer_index, 0] * low_back(patch_mixed)
        normed = low(aff_scale[current_layer_index, 1] * middle + aff_shift[current_layer_index, 1])
        summed = jnp.zeros_like(middle)
        for group_index in range(N_HID):
            first_col = group_index * group_width
            w_in = fc1_weight[current_layer_index][:, first_col:first_col + group_width]
            w_out = fc2_weight[current_layer_index][:, first_col:first_col + group_width]
            before_activation = jnp.einsum('bpd,df->bpf', low_back(normed), w_in, precision=FULL_ACCURACY)
            before_activation = before_activation + fc1_bias[current_layer_index][first_col:first_col + group_width]
            activated = low(gelu_exact(low_back(before_activation)))
            summed = summed + low(jnp.einsum('bpf,df->bpd', activated, w_out, precision=FULL_ACCURACY))
        stream = middle + layer_scale[current_layer_index, 1] * low_back(summed + fc2_bias[current_layer_index])
    return stream

def reference(tokens, masks, cotangent, aff_scale, aff_shift, layer_scale, crosspatch_weight, cross_bias, fc1_weight, fc1_bias, fc2_weight, fc2_bias):
    params = tuple((array_in.astype(jnp.float32) for array_in in (aff_scale, aff_shift, layer_scale, crosspatch_weight, cross_bias, fc1_weight, fc1_bias, fc2_weight, fc2_bias)))
    block_count = IMAGES // IMG_DEV
    token_blocks = tokens.astype(jnp.float32).reshape(block_count, IMG_DEV, PATCHES, D)
    mask_blocks = masks.astype(jnp.float32).reshape(block_count, IMG_DEV, PATCHES, 1)
    cot_blocks = cotangent.astype(jnp.float32).reshape(block_count, IMG_DEV, PATCHES, D)

    def block_step(carried, inputs):
        token_block, mask_block, cot_block = inputs

        def forward(params_in, stream):
            return layer_stack(params_in, stream, mask_block)
        result, pullback = jax.vjp(forward, params, token_block)
        param_grads, token_grad = pullback(cot_block)
        carried = jax.tree.map(lambda running, addend: running + addend, carried, param_grads)
        return (carried, (result.astype(jnp.bfloat16), token_grad.astype(jnp.bfloat16)))
    zeros_init = jax.tree.map(jnp.zeros_like, params)
    grads, (results, token_grads) = lax.scan(block_step, zeros_init, (token_blocks, mask_blocks, cot_blocks))
    return (results.reshape(IMAGES, PATCHES, D), token_grads.reshape(IMAGES, PATCHES, D), grads[0], grads[1], grads[2], grads[3], grads[4], grads[5], grads[6], grads[7], grads[8])
```

```python
import functools

import jax
import jax.numpy as jnp
from jax import lax
from jax.experimental import pallas as pl
from jax.experimental.pallas import tpu as pltpu
from jax.sharding import PartitionSpec as P

BF = jnp.bfloat16
F32 = jnp.float32
NN = (((1,), (0,)), ((), ()))
NT = (((1,), (1,)), ((), ()))
TN = (((0,), (0,)), ((), ()))
SQRT_HALF = 0.7071067811865476
PDF_SCALE = 0.3989422804014327
S0, T0, S1, T1, LS0, LS1, B2, B1 = range(8)


def dot(a, b, dims):
    return lax.dot_general(a, b, dims, preferred_element_type=F32)


def partial_rows(v):
    return jnp.sum(v.reshape(v.shape[0] // 8, 8, v.shape[1]), axis=0)


def fused_kernel(
    cfg,
    own_ref,
    tok_ref,
    keep_ref,
    cot_ref,
    scale_ref,
    shift_ref,
    ls_ref,
    wc_ref,
    w1_ref,
    b1_ref,
    w2_ref,
    b2_ref,
    out_ref,
    tgrad_ref,
    w1g_ref,
    w2g_ref,
    cwg_ref,
    sums_ref,
    x_s,
    mid_s,
    grad_s,
    mixed_s,
    crossed_s,
    normed_s,
    h_s,
    phi_s,
    act_s,
    branch_s,
    bg_s,
    pg_s,
    cg_s,
):
    layers, patches, rows, images, width, own_width = cfg
    step = pl.program_id(0)
    whole = patches // 16 * 16
    pair = 2 * rows
    blocks = [slice(r, min(r + pair, images * rows)) for r in range(0, images * rows, pair)]

    @pl.when(step == 0)
    def _():
        for ref in (w1g_ref, w2g_ref, cwg_ref, sums_ref, x_s, grad_s):
            ref[...] = jnp.zeros_like(ref)

    own = pl.ds(pl.multiple_of(own_ref[0] * own_width, 128), own_width)
    lane = lax.broadcasted_iota(jnp.int32, (1, rows), 1)

    def row(ref, l, k):
        return ref[l, k : k + 1, :]

    def image(g):
        return slice(g * rows, (g + 1) * rows)

    def add(l, kind, value):
        sums_ref[l, kind] += partial_rows(value)

    def keep_of(g):
        return keep_ref[g]

    for g in range(images):
        x_s[0, g * rows : g * rows + patches, :] = tok_ref[g].astype(F32)
    for l in range(layers):
        for g in range(images):
            at = image(g)
            x = x_s[l, at, :]
            mixed = x * row(scale_ref, l, 0) + row(shift_ref, l, 0)
            mixed_s[l, g * rows : g * rows + whole, :] = mixed[:whole].astype(BF)
            tail = lax.broadcasted_iota(jnp.int32, (rows - whole, 1), 0) + whole
            mixed_s[l, g * rows + whole : (g + 1) * rows, :] = jnp.where(
                tail < patches, mixed[whole:], 1.0
            ).astype(BF)
            wk = wc_ref[l] * jnp.where(lane < patches, keep_of(g), 1.0).astype(BF)
            crossed = dot(wk, mixed_s[l, at, :], NN)
            crossed_s[l, at, :] = crossed.astype(BF)
            middle = x + row(ls_ref, l, 0) * crossed
            mid_s[l, at, :] = middle
            normed_s[l, at, :] = (middle * row(scale_ref, l, 1) + row(shift_ref, l, 1)).astype(BF)
        for at in blocks:
            h = dot(normed_s[l, at, :], w1_ref[l], NN) + b1_ref[l : l + 1, :]
            phi = 0.5 + 0.5 * lax.erf(h * SQRT_HALF)
            act_s[l, at, :] = (h * phi).astype(BF)
            h_s[l, at, :] = h.astype(BF)
            phi_s[l, at, :] = phi.astype(BF)
        for at in blocks:
            branch = dot(act_s[l, at, :], w2_ref[l], NT) + b2_ref[l : l + 1, :]
            branch_s[l, at, :] = branch.astype(BF)
            x_s[l + 1, at, :] = mid_s[l, at, :] + row(ls_ref, l, 1) * branch
    for g in range(images):
        out_ref[g] = x_s[layers, g * rows : g * rows + patches, :].astype(BF)
        grad_s[g * rows : g * rows + patches, :] = cot_ref[g].astype(F32)

    for l in reversed(range(layers)):
        for at in blocks:
            grad = grad_s[at, :]
            add(l, LS1, grad * branch_s[l, at, :].astype(F32))
            bg = row(ls_ref, l, 1) * grad
            add(l, B2, bg)
            bg_s[at, :] = bg.astype(BF)
        for at in blocks:
            act_grad = dot(bg_s[at, :], w2_ref[l], NN)
            h = h_s[l, at, :].astype(F32)
            slope = phi_s[l, at, :].astype(F32) + h * (jnp.exp(h * h * -0.5) * PDF_SCALE)
            pg_s[at, :] = (act_grad * slope).astype(BF)
        add(l, B1, pg_s[:, own].astype(F32))
        w1g_ref[l] += dot(normed_s[l], pg_s[:, own], TN)
        w2g_ref[l] += dot(bg_s[...], act_s[l, :, own], TN)
        for at in blocks:
            normed_grad = dot(pg_s[at, :], w1_ref[l], NT)
            middle = mid_s[l, at, :]
            add(l, S1, normed_grad * middle)
            add(l, T1, normed_grad)
            middle_grad = grad_s[at, :] + row(scale_ref, l, 1) * normed_grad
            add(l, LS0, middle_grad * crossed_s[l, at, :].astype(F32))
            grad_s[at, :] = middle_grad
            cg_s[at, :] = (row(ls_ref, l, 0) * middle_grad).astype(BF)
        for g in range(images):
            at = image(g)
            keep = keep_of(g)
            cg = cg_s[at, :]
            cwg_ref[l] += dot(cg, mixed_s[l, at, :], NT) * jnp.where(lane < patches, keep, 1.0)
            wk = wc_ref[l] * jnp.where(lane < patches, keep, 0.0).astype(BF)
            mixed_grad = dot(wk, cg, TN)
            add(l, S0, mixed_grad * x_s[l, at, :])
            add(l, T0, mixed_grad)
            grad_s[at, :] += row(scale_ref, l, 0) * mixed_grad
    for g in range(images):
        tgrad_ref[g] = grad_s[g * rows : g * rows + patches, :].astype(BF)


def fused(own, tokens, keep, cotangent, scale, shift, ls, wc, w1, b1, w2, b2, images, own_width):
    count, patches, width = tokens.shape
    layers, _, hidden = w1.shape
    rows = (patches + 15) // 16 * 16
    steps = count // images
    m = images * rows
    vmem = pl.BlockSpec(memory_space=pltpu.VMEM)
    per_chunk = pl.BlockSpec((images, patches, width), lambda i: (i, 0, 0))

    def whole_block(shape):
        return pl.BlockSpec(shape, lambda i: (0,) * len(shape))

    wg = (layers, width, own_width)
    cw = (layers, rows, rows)
    sm = (layers, 8, 8, width)
    flops = count * rows * (12 * width * hidden + 6 * rows * width) * layers
    return pl.pallas_call(
        functools.partial(fused_kernel, (layers, patches, rows, images, width, own_width)),
        grid=(steps,),
        in_specs=[
            pl.BlockSpec(memory_space=pltpu.SMEM),
            per_chunk,
            pl.BlockSpec((images, 1, rows), lambda i: (i, 0, 0)),
            per_chunk,
        ]
        + [vmem] * 8,
        out_specs=[
            per_chunk,
            per_chunk,
            whole_block(wg),
            whole_block(wg),
            whole_block(cw),
            whole_block(sm),
        ],
        out_shape=[
            jax.ShapeDtypeStruct(tokens.shape, BF),
            jax.ShapeDtypeStruct(tokens.shape, BF),
            jax.ShapeDtypeStruct(wg, F32),
            jax.ShapeDtypeStruct(wg, F32),
            jax.ShapeDtypeStruct(cw, F32),
            jax.ShapeDtypeStruct(sm, F32),
        ],
        scratch_shapes=[
            pltpu.VMEM((layers + 1, m, width), F32),
            pltpu.VMEM((layers, m, width), F32),
            pltpu.VMEM((m, width), F32),
            pltpu.VMEM((layers, m, width), BF),
            pltpu.VMEM((layers, m, width), BF),
            pltpu.VMEM((layers, m, width), BF),
            pltpu.VMEM((layers, m, hidden), BF),
            pltpu.VMEM((layers, m, hidden), BF),
            pltpu.VMEM((layers, m, hidden), BF),
            pltpu.VMEM((layers, m, width), BF),
            pltpu.VMEM((m, width), BF),
            pltpu.VMEM((m, hidden), BF),
            pltpu.VMEM((m, width), BF),
        ],
        compiler_params=pltpu.CompilerParams(vmem_limit_bytes=60 * 2**20),
        cost_estimate=pl.CostEstimate(
            flops=flops, bytes_accessed=4 * tokens.size * 2, transcendentals=0
        ),
    )(own, tokens, keep, cotangent, scale, shift, ls, wc, w1, b1, w2, b2)


def on_device(
    tokens,
    masks,
    cotangent,
    aff_scale,
    aff_shift,
    layer_scale,
    crosspatch_weight,
    cross_bias,
    fc1_weight,
    fc1_bias,
    fc2_weight,
    fc2_bias,
):
    count, patches, width = tokens.shape
    layers, shard, own_width = fc1_weight.shape
    rows = (patches + 15) // 16 * 16
    n_dp = lax.axis_size("dp")
    own = lax.axis_index("hid").reshape(1)

    def whole(w):
        w = lax.all_gather(w, "hid", axis=2, tiled=True)
        return lax.all_gather(w, "dp", axis=1, tiled=True)

    w1, w2 = whole(fc1_weight), whole(fc2_weight)
    bias_hi = cross_bias.astype(BF)
    bias_lo = (cross_bias - bias_hi.astype(F32)).astype(BF)
    wc = jnp.concatenate([crosspatch_weight, bias_hi[:, :, None], bias_lo[:, :, None]], axis=2)
    wc = jnp.pad(wc, ((0, 0), (0, rows - patches), (0, rows - patches - 2)))
    keep = jnp.pad(masks.astype(F32)[:, None, :], ((0, 0), (0, 0), (0, rows - patches)))

    out, tgrad, w1g, w2g, cwg, sums = fused(
        own,
        tokens,
        keep,
        cotangent,
        aff_scale,
        aff_shift,
        layer_scale,
        wc,
        w1,
        fc1_bias,
        w2,
        fc2_bias,
        4,
        own_width,
    )

    both = jnp.stack([w1g, w2g]).astype(BF).reshape(2, layers, n_dp, shard, own_width)
    both = jnp.moveaxis(both, 2, 0)
    both = lax.all_to_all(both, "dp", split_axis=0, concat_axis=0, tiled=True)
    both = both.astype(F32).sum(axis=0)
    sums = sums.sum(axis=2)
    cwg, sums = lax.psum((cwg, sums), "dp")
    return (
        out,
        tgrad,
        jnp.stack([sums[:, S0], sums[:, S1]], axis=1),
        jnp.stack([sums[:, T0], sums[:, T1]], axis=1),
        jnp.stack([sums[:, LS0], sums[:, LS1]], axis=1),
        cwg[:, :patches, :patches],
        cwg[:, :patches, patches],
        both[0],
        sums[:, B1],
        both[1],
        sums[:, B2],
    )


def solution(mesh):
    return jax.shard_map(
        on_device,
        mesh=mesh,
        in_specs=(
            P("dp", None, None),
            P("dp", None),
            P("dp", None, None),
            P(),
            P(),
            P(),
            P(),
            P(),
            P(None, "dp", "hid"),
            P(),
            P(None, "dp", "hid"),
            P(),
        ),
        out_specs=(
            P("dp", None, None),
            P("dp", None, None),
            P(),
            P(),
            P(),
            P(),
            P(),
            P(None, "dp", "hid"),
            P(None, "hid"),
            P(None, "dp", "hid"),
            P(),
        ),
        check_vma=False,
    )
```

```python
import functools

import jax
import jax.numpy as jnp
from jax import lax
from jax.experimental import pallas as pl
from jax.experimental.pallas import tpu as pltpu
from jax.sharding import PartitionSpec as P

BF = jnp.bfloat16
F32 = jnp.float32
NN = (((1,), (0,)), ((), ()))
NT = (((1,), (1,)), ((), ()))
TN = (((0,), (0,)), ((), ()))
SQRT_HALF = 0.7071067811865476
PDF_SCALE = 0.3989422804014327
S0, T0, S1, T1, LS0, LS1, B2, B1 = range(8)
STEP = 4
ALONE = 8


def dot(a, b, dims):
    return lax.dot_general(a, b, dims, preferred_element_type=F32)


def round_up(n, k):
    return (n + k - 1) // k * k


class Sizes:
    def __init__(self, tokens, fc1, n_dp, n_hid):
        self.count, self.patches, self.width = tokens.shape
        self.layers, self.shard, self.own = fc1.shape
        self.n_dp, self.n_hid = n_dp, n_hid
        self.hidden = self.own * n_hid
        self.rows = round_up(self.patches, 8)
        self.depth = round_up(self.patches + 2, 16)
        self.m = STEP * self.rows
        self.small = self.rows + 16
        self.blocks = self.shard % 16 == 0 and self.own % 128 == 0


def kernel_body(sz, kept, names, *args):
    r = dict(zip(names, args))
    meta = r["meta"]
    step = pl.program_id(0)
    last = pl.num_programs(0) - 1
    layers, rows, patches, depth, m = sz.layers, sz.rows, sz.patches, sz.depth, sz.m
    alone = kept != sz.own
    whole = patches // 16 * 16
    pair = 2 * rows
    blocks = [slice(i, min(i + pair, m)) for i in range(0, m, pair)]
    lane = lax.broadcasted_iota(jnp.int32, (1, depth), 1)
    columns = pl.ds(pl.multiple_of(meta[1] * kept, 128), kept)
    mine = pl.ds(pl.multiple_of(meta[2] * sz.own, 128), sz.own)
    theirs = pl.ds(pl.multiple_of(meta[3] * sz.own, 128), sz.own)
    x, grad, gw = r["x"], r["grad"], r["gw"]

    @pl.when(step == 0)
    def _():
        if sz.blocks:
            for l in range(layers):
                for i in range(2):
                    for half in range(2):
                        src = r[f"w{i}part{half}_{l}"]
                        n_part = src.shape[0]
                        for k in range(n_part):
                            at = meta[4 + i * sz.n_dp + half * n_part + k] * sz.shard
                            at = pl.ds(pl.multiple_of(at, 16), sz.shard)
                            for j in range(sz.n_hid):
                                to = meta[4 + 2 * sz.n_dp + j] * sz.own
                                to = pl.ds(pl.multiple_of(to, 128), sz.own)
                                pltpu.make_async_copy(
                                    src.at[k, j], r["w"].at[i, l, at, to], r["arrive"].at[i, l]
                                ).start()
        for name in ("gwc", "gsum", "gb1"):
            r[name][...] = jnp.zeros_like(r[name])
        x[0] = jnp.zeros_like(x[0])
        grad[...] = jnp.zeros_like(grad)
        if alone:
            gw[...] = jnp.zeros_like(gw)
        else:
            pltpu.make_async_copy(r["carry"], gw, r["carried"]).start()

    def weight_ready(i, l):
        if sz.blocks:

            @pl.when(step == 0)
            def _():
                ref = r["w"].at[i, l]
                pltpu.make_async_copy(ref, ref, r["arrive"].at[i, l]).wait()

    def weight(i, l):
        return r["w"][i, l] if sz.blocks else r[f"w{i}_{l}"][...]

    def row(name, l, k):
        return r[name][l, k : k + 1, :]

    def image(g):
        return slice(g * rows, (g + 1) * rows)

    def add(l, kind, v):
        r["gsum"][l, kind] += jnp.sum(v.reshape(v.shape[0] // 8, 8, v.shape[1]), axis=0)

    for g in range(STEP):
        x[0, g * rows : g * rows + patches, :] = r["tok"][g].astype(F32)
    for l in range(layers):
        mid, mixed, crossed = r["mid"], r["mixed"], r["crossed"]
        for g in range(STEP):
            x_in = x[l, image(g), :]
            v = x_in * row("scale", l, 0) + row("shift", l, 0)
            mixed[l, g, :whole, :] = v[:whole].astype(BF)
            left = lax.broadcasted_iota(jnp.int32, (rows - whole, 1), 0) + whole
            tail = jnp.where(left < patches, v[whole:], 1.0)
            if depth > rows:
                tail = jnp.concatenate([tail, jnp.ones((depth - rows, sz.width), F32)], axis=0)
            mixed[l, g, whole:, :] = tail.astype(BF)
            wk = r["wc"][l] * jnp.where(lane < patches, r["keep"][g], 1.0).astype(BF)
            c = dot(wk, mixed[l, g], NN)
            crossed[l, g, :rows, :] = c.astype(BF)
            mid[l, image(g), :] = x_in + row("ls", l, 0) * c
        for at in blocks:
            v = mid[l, at, :] * row("scale", l, 1) + row("shift", l, 1)
            r["normed"][l, at, :] = v.astype(BF)
        weight_ready(0, l)
        for at in blocks:
            h = dot(r["normed"][l, at, :], weight(0, l), NN) + r["b1"][l : l + 1, :]
            phi = 0.5 + 0.5 * lax.erf(h * SQRT_HALF)
            r["act"][l, at, :] = (h * phi).astype(BF)
            r["h"][l, at, :] = h.astype(BF)
            r["phi"][l, at, :] = phi.astype(BF)
        weight_ready(1, l)
        for at in blocks:
            branch = dot(r["act"][l, at, :], weight(1, l), NT) + r["b2"][l : l + 1, :]
            r["branch"][l, at, :] = branch.astype(BF)
            x[l + 1, at, :] = mid[l, at, :] + row("ls", l, 1) * branch
    for g in range(STEP):
        inside = slice(g * rows, g * rows + patches)
        r["out"][g] = x[layers, inside, :].astype(BF)
        grad[inside, :] = r["cot"][g].astype(F32)

    if not alone:

        @pl.when(step == 0)
        def _():
            pltpu.make_async_copy(r["carry"], gw, r["carried"]).wait()

    for l in reversed(range(layers)):
        for at in blocks:
            g_out = grad[at, :]
            add(l, LS1, g_out * r["branch"][l, at, :].astype(F32))
            bg = row("ls", l, 1) * g_out
            add(l, B2, bg)
            r["bg"][at, :] = bg.astype(BF)
        for at in blocks:
            act_grad = dot(r["bg"][at, :], weight(1, l), NN)
            h = r["h"][l, at, :].astype(F32)
            slope = r["phi"][l, at, :].astype(F32) + h * (jnp.exp(h * h * -0.5) * PDF_SCALE)
            r["pg"][at, :] = (act_grad * slope).astype(BF)
        pg = r["pg"][:, columns]
        r["gb1"][l] += jnp.sum(pg.astype(F32).reshape(m // 8, 8, kept), axis=0)
        gw[0, l] += dot(r["normed"][l], pg, TN)
        gw[1, l] += dot(r["bg"][...], r["act"][l, :, columns], TN)
        for at in blocks:
            normed_grad = dot(r["pg"][at, :], weight(0, l), NT)
            add(l, S1, normed_grad * r["mid"][l, at, :])
            add(l, T1, normed_grad)
            grad[at, :] += row("scale", l, 1) * normed_grad
        for g in range(STEP):
            at = image(g)
            keep = r["keep"][g]
            mg = grad[at, :]
            add(l, LS0, mg * r["crossed"][l, g, :rows, :].astype(F32))
            cg = (row("ls", l, 0) * mg).astype(BF)
            r["gwc"][l] += dot(cg, r["mixed"][l, g], NT) * jnp.where(lane < patches, keep, 1.0)
            wk = r["wc"][l] * jnp.where(lane < patches, keep, 0.0).astype(BF)
            mixed_grad = dot(wk, cg, TN)[:rows]
            add(l, S0, mixed_grad * x[l, at, :])
            add(l, T0, mixed_grad)
            grad[at, :] = mg + row("scale", l, 0) * mixed_grad
    for g in range(STEP):
        r["tgrad"][g] = grad[g * rows : g * rows + patches, :].astype(BF)

    @pl.when(step == last)
    def _():
        def write_small(ref, wanted):
            for l in range(layers):
                sums = [jnp.sum(r["gsum"][l, k], axis=0, keepdims=True) for k in range(B1)]
                sums.append(jnp.sum(r["gb1"][l, :, wanted], axis=0, keepdims=True))
                table = jnp.concatenate(sums, axis=0)
                table = jnp.pad(table, ((0, 0), (0, 512 - sz.width)))
                gwc = jnp.pad(r["gwc"][l], ((0, 0), (0, 256 - depth)))
                full = jnp.concatenate([gwc, table[:, :256], table[:, 256:]], axis=0)
                ref[l] = full.astype(BF)

        def write_blocks(ref, wanted):
            for i in range(2):
                for l in range(layers):
                    v = gw[i, l, :, wanted].astype(BF)
                    if sz.blocks:
                        for k in range(sz.n_dp):
                            ref[k, i, l] = v[k * sz.shard : (k + 1) * sz.shard]
                    else:
                        ref[i, l] = v

        if alone:
            write_small(r["small"], mine)
            write_small(r["send"], theirs)
            write_blocks(r["blocks"], theirs)
            for i in range(2):
                for l in range(layers):
                    r["own"][i, l] = gw[i, l, :, mine]
        else:
            write_small(r["small"], slice(None))
            write_blocks(r["blocks"], slice(None))


def run(sz, steps, alone, meta, common, weights, carry=None):
    w, m, layers = sz.width, sz.m, sz.layers
    kept = 2 * sz.own if alone else sz.own
    vmem = pl.BlockSpec(memory_space=pltpu.VMEM)
    anywhere = pl.BlockSpec(memory_space=pl.ANY)
    images = (STEP, sz.patches, w)

    def spec(block, where):
        return pl.BlockSpec(block, lambda i, meta: (where(i, meta),) + (0,) * (len(block) - 1))

    def in_all(i, meta):
        return meta[0] + i

    def in_part(i, meta):
        return i

    def fixed(i, meta):
        return 0

    ins = [
        ("tok", common["tok"], spec(images, in_all)),
        ("cot", common["cot"], spec(images, in_all)),
        ("keep", common["keep"], spec((STEP, 1, sz.depth), in_all)),
    ]
    for name in ("scale", "shift", "ls", "wc", "b1", "b2"):
        ins.append((name, common[name], vmem))
    scratch = []
    for l in range(layers):
        for i in range(2):
            if sz.blocks:
                for half in range(2):
                    ins.append((f"w{i}part{half}_{l}", weights[l][i][half], anywhere))
            else:
                ins.append((f"w{i}_{l}", weights[l][i], vmem))
    if sz.blocks:
        scratch.append(("w", pltpu.VMEM((2, layers, w, sz.hidden), BF)))
        scratch.append(("arrive", pltpu.SemaphoreType.DMA((2, layers))))
    if not alone:
        ins.append(("carry", carry, anywhere))
        scratch.append(("carried", pltpu.SemaphoreType.DMA))

    where, count = (in_part, steps * STEP) if alone else (in_all, sz.count)
    outs = [
        ("out", (count,) + images[1:], BF, spec(images, where)),
        ("tgrad", (count,) + images[1:], BF, spec(images, where)),
    ]
    small = (layers, sz.small, 256)
    block = (sz.n_dp, 2, layers, sz.shard, sz.own) if sz.blocks else (2, layers, w, sz.own)
    outs.append(("small", small, BF, spec(small, fixed)))
    outs.append(("blocks", block, BF, spec(block, fixed)))
    if alone:
        outs.append(("send", small, BF, spec(small, fixed)))
        own = (2, layers, w, sz.own)
        outs.append(("own", own, F32, spec(own, fixed)))
    for name, shape, dtype in (
        ("x", (layers + 1, m, w), F32),
        ("mid", (layers, m, w), F32),
        ("crossed", (layers, STEP, sz.depth, w), BF),
        ("mixed", (layers, STEP, sz.depth, w), BF),
        ("normed", (layers, m, w), BF),
        ("h", (layers, m, sz.hidden), BF),
        ("phi", (layers, m, sz.hidden), BF),
        ("act", (layers, m, sz.hidden), BF),
        ("branch", (layers, m, w), BF),
        ("grad", (m, w), F32),
        ("bg", (m, w), BF),
        ("pg", (m, sz.hidden), BF),
        ("gw", (2, layers, w, kept), F32),
        ("gwc", (layers, sz.rows, sz.depth), F32),
        ("gsum", (layers, B1, 8, w), F32),
        ("gb1", (layers, 8, kept), F32),
    ):
        scratch.append((name, pltpu.VMEM(shape, dtype)))
    names = ("meta",) + tuple(e[0] for e in ins + outs + scratch)
    flops = steps * m * 24 * w * sz.hidden
    results = pl.pallas_call(
        functools.partial(kernel_body, sz, kept, names),
        grid_spec=pltpu.PrefetchScalarGridSpec(
            num_scalar_prefetch=1,
            grid=(steps,),
            in_specs=[e[2] for e in ins],
            out_specs=[e[3] for e in outs],
            scratch_shapes=[e[1] for e in scratch],
        ),
        out_shape=[jax.ShapeDtypeStruct(e[1], e[2]) for e in outs],
        compiler_params=pltpu.CompilerParams(vmem_limit_bytes=60 * 2**20),
        cost_estimate=pl.CostEstimate(flops=flops, bytes_accessed=flops // 400, transcendentals=0),
    )(meta, *[e[1] for e in ins])
    return {e[0]: value for e, value in zip(outs, results)}


def swap(x, axis, k):
    n = lax.axis_size(axis)
    return lax.ppermute(x, axis, [(i, i ^ k) for i in range(n)])


def powers(n):
    return [2**k for k in range(1, n.bit_length() - 1)]


def gather_weights(sz, w1, w2):
    both = jnp.stack([w1, w2])
    parts = [both] + [swap(both, "hid", k) for k in range(1, sz.n_hid)]
    got = [jnp.stack([p[i] for p in parts])[None] for i in range(2)]
    bits = powers(sz.n_dp)
    for step in range(len(bits)):
        moved = [swap(got[0], "dp", bits[step]), swap(got[1], "dp", bits[-1 - step])]
        got = [jnp.concatenate([g, v]) for g, v in zip(got, moved)]
    other = [swap(g, "dp", 1) for g in got]
    orders = []
    for seq in (bits, bits[::-1]):
        order = [0]
        for b in seq:
            order += [o ^ b for o in order]
        orders.append(order + [o ^ 1 for o in order])
    return got, other, orders


def on_device(
    tokens,
    masks,
    cotangent,
    aff_scale,
    aff_shift,
    layer_scale,
    crosspatch_weight,
    cross_bias,
    fc1_weight,
    fc1_bias,
    fc2_weight,
    fc2_bias,
):
    n_dp, n_hid = lax.axis_size("dp"), lax.axis_size("hid")
    sz = Sizes(tokens, fc1_weight, n_dp, n_hid)
    layers, patches = sz.layers, sz.patches
    me, hid = lax.axis_index("dp"), lax.axis_index("hid")
    half = hid % 2

    weights = []
    for l in range(layers):
        got, other, orders = gather_weights(sz, fc1_weight[l], fc2_weight[l])
        if sz.blocks:
            weights.append([(got[i], other[i]) for i in range(2)])
        else:
            ready = []
            for i in range(2):
                w = jnp.concatenate([got[i], other[i]])
                at = jnp.zeros(n_dp, jnp.int32).at[jnp.array(orders[i])].set(jnp.arange(n_dp))
                w = w[at[jnp.arange(n_dp) ^ me]][:, jnp.arange(n_hid) ^ hid]
                ready.append(w.transpose(0, 2, 1, 3).reshape(sz.width, sz.hidden))
            weights.append(ready)

    bias_hi = cross_bias.astype(BF)
    bias_lo = (cross_bias - bias_hi.astype(F32)).astype(BF)
    wc = jnp.concatenate([crosspatch_weight, bias_hi[:, :, None], bias_lo[:, :, None]], axis=2)
    wc = jnp.pad(wc, ((0, 0), (0, sz.rows - patches), (0, sz.depth - patches - 2)))
    keep = jnp.pad(masks.astype(F32)[:, None, :], ((0, 0), (0, 0), (0, sz.depth - patches)))
    common = {
        "tok": tokens,
        "cot": cotangent,
        "keep": keep,
        "scale": aff_scale,
        "shift": aff_shift,
        "ls": layer_scale,
        "wc": wc,
        "b1": fc1_bias,
        "b2": fc2_bias,
    }
    groups = ALONE // STEP
    shared = sz.count // STEP - 2 * groups
    places = [me ^ k for k in orders[0] + orders[1]] + [hid ^ j for j in range(n_hid)]

    def meta(first, column):
        return jnp.stack([first, column, half, 1 - half] + places).astype(jnp.int32)

    first = run(sz, groups, True, meta(half * groups, hid // 2), common, weights)
    sent_out = swap(first["out"], "hid", 1)
    sent_grad = swap(first["tgrad"], "hid", 1)
    sent_small = swap(first["send"], "hid", 1)

    def to_owners(blocks):
        if not sz.blocks:
            blocks = blocks.reshape(2, layers, n_dp, sz.shard, sz.own)
            blocks = jnp.moveaxis(blocks, 2, 0)
        got = lax.all_to_all(blocks, "dp", split_axis=0, concat_axis=0, tiled=True)
        return got.astype(F32).sum(axis=0)

    theirs = swap(to_owners(first["blocks"]).astype(BF), "hid", 1)
    rest = run(
        sz, shared, False, meta(jnp.int32(2 * groups), hid), common, weights, first["own"]
    )
    gw = to_owners(rest["blocks"]) + theirs.astype(F32)

    alone_small = first["small"].astype(F32) + sent_small.astype(F32)
    small = (alone_small + rest["small"].astype(F32)).astype(BF)
    small = [lax.all_gather(small[l], "dp").astype(F32).sum(axis=0) for l in range(layers)]
    small = jnp.stack(small)
    gwc = small[:, :patches, :patches]
    sums = jnp.concatenate(
        [small[:, sz.rows : sz.rows + 8], small[:, sz.rows + 8 :, : sz.width - 256]], axis=2
    )

    def put(all_images, mine, theirs):
        all_images = lax.dynamic_update_slice_in_dim(all_images, mine, half * ALONE, axis=0)
        return lax.dynamic_update_slice_in_dim(all_images, theirs, (1 - half) * ALONE, axis=0)

    return (
        put(rest["out"], first["out"], sent_out),
        put(rest["tgrad"], first["tgrad"], sent_grad),
        jnp.stack([sums[:, S0], sums[:, S1]], axis=1),
        jnp.stack([sums[:, T0], sums[:, T1]], axis=1),
        jnp.stack([sums[:, LS0], sums[:, LS1]], axis=1),
        gwc,
        small[:, :patches, patches],
        gw[0],
        sums[:, B1],
        gw[1],
        sums[:, B2],
    )


def solution(mesh):
    return jax.shard_map(
        on_device,
        mesh=mesh,
        in_specs=(
            P("dp", None, None),
            P("dp", None),
            P("dp", None, None),
            P(),
            P(),
            P(),
            P(),
            P(),
            P(None, "dp", "hid"),
            P(),
            P(None, "dp", "hid"),
            P(),
        ),
        out_specs=(
            P("dp", None, None),
            P("dp", None, None),
            P(),
            P(),
            P(),
            P(),
            P(),
            P(None, "dp", "hid"),
            P(None, "hid"),
            P(None, "dp", "hid"),
            P(),
        ),
        check_vma=False,
    )
```

```python
import functools

import jax
import jax.numpy as jnp
from jax import lax
from jax.experimental import pallas as pl
from jax.experimental.pallas import tpu as pltpu
from jax.sharding import PartitionSpec as P

BF = jnp.bfloat16
F32 = jnp.float32
NN = (((1,), (0,)), ((), ()))
NT = (((1,), (1,)), ((), ()))
TN = (((0,), (0,)), ((), ()))
SQRT_HALF = 0.7071067811865476
PDF_SCALE = 0.3989422804014327
S0, T0, S1, T1, LS0, LS1, B2, B1 = range(8)
STEP = 4
GROUP = 8


def dot(a, b, dims):
    return lax.dot_general(a, b, dims, preferred_element_type=F32)


def round_up(n, k):
    return (n + k - 1) // k * k


class Sizes:
    def __init__(self, tokens, fc1, n_dp, n_hid):
        self.count, self.patches, self.width = tokens.shape
        self.layers, self.shard, self.own = fc1.shape
        self.n_dp, self.n_hid = n_dp, n_hid
        self.hidden = self.own * n_hid
        self.rows = round_up(self.patches, 8)
        self.depth = round_up(self.patches + 2, 16)
        self.m = STEP * self.rows
        self.small = self.rows + 16
        self.blocks = self.shard % 16 == 0 and self.own % 128 == 0


def kernel_body(sz, kept, names, *args):
    r = dict(zip(names, args))
    meta = r["meta"]
    step = pl.program_id(0)
    last = pl.num_programs(0) - 1
    layers, rows, patches, depth, m = sz.layers, sz.rows, sz.patches, sz.depth, sz.m
    alone = kept != sz.own
    whole = patches // 16 * 16
    pair = 2 * rows
    blocks = [slice(i, min(i + pair, m)) for i in range(0, m, pair)]
    lane = lax.broadcasted_iota(jnp.int32, (1, depth), 1)
    columns = pl.ds(pl.multiple_of(meta[1] * kept, 128), kept)
    mine = pl.ds(pl.multiple_of(meta[2] * sz.own, 128), sz.own)
    theirs = pl.ds(pl.multiple_of(meta[3] * sz.own, 128), sz.own)
    x, grad, gw = r["x"], r["grad"], r["gw"]

    @pl.when(step == 0)
    def _():
        if sz.blocks:
            for l in range(layers):
                for i in range(2):
                    for half in range(2):
                        src = r[f"w{i}part{half}_{l}"]
                        n_part = src.shape[0]
                        for k in range(n_part):
                            at = meta[4 + i * sz.n_dp + half * n_part + k] * sz.shard
                            at = pl.ds(pl.multiple_of(at, 16), sz.shard)
                            pltpu.make_async_copy(
                                src.at[k], r["w"].at[i, l, at], r["arrive"].at[i, l]
                            ).start()
        for name in ("gwc", "gsum", "gb1"):
            r[name][...] = jnp.zeros_like(r[name])
        for name in ("tok", "cot"):
            staged = r[name + "f"]
            for c in range(sz.width // 128):
                part = r[name][:, :, c * 128 : (c + 1) * 128].astype(F32)
                staged[c, : patches * GROUP, :] = part.reshape(patches * GROUP, 128)
                staged[c, patches * GROUP :, :] = jnp.zeros(((rows - patches) * GROUP, 128), F32)
        if alone:
            gw[...] = jnp.zeros_like(gw)
        else:
            pltpu.make_async_copy(r["carry"], gw, r["carried"]).start()

    def weight_ready(i, l):
        if sz.blocks:

            @pl.when(step == 0)
            def _():
                ref = r["w"].at[i, l]
                pltpu.make_async_copy(ref, ref, r["arrive"].at[i, l]).wait()

    def weight(i, l):
        return r["w"][i, l]

    def row(name, l, k):
        return r[name][l, k : k + 1, :]

    def image(g):
        return slice(g * rows, (g + 1) * rows)

    def add(l, kind, v):
        r["gsum"][l, kind] += jnp.sum(v.reshape(v.shape[0] // 8, 8, v.shape[1]), axis=0)

    def unstage(name, g):
        at = pl.ds(step * STEP + g, rows, stride=GROUP)
        return jnp.concatenate([r[name][c, at, :] for c in range(sz.width // 128)], axis=1)

    def stage(name, g, v):
        at = pl.ds(step * STEP + g, rows, stride=GROUP)
        for c in range(sz.width // 128):
            r[name][c, at, :] = v[:, c * 128 : (c + 1) * 128]

    for g in range(STEP):
        x[0, image(g), :] = unstage("tokf", g)
    def forward(l, _):
        mid, mixed, crossed = r["mid"], r["mixed"], r["crossed"]
        for g in range(STEP):
            x_in = x[l, image(g), :]
            v = x_in * row("scale", l, 0) + row("shift", l, 0)
            mixed[l, g, :whole, :] = v[:whole].astype(BF)
            left = lax.broadcasted_iota(jnp.int32, (rows - whole, 1), 0) + whole
            tail = jnp.where(left < patches, v[whole:], 1.0)
            if depth > rows:
                tail = jnp.concatenate([tail, jnp.ones((depth - rows, sz.width), F32)], axis=0)
            mixed[l, g, whole:, :] = tail.astype(BF)
            wk = r["wc"][l] * jnp.where(lane < patches, r["keep"][g], 1.0).astype(BF)
            c = dot(wk, mixed[l, g], NN)
            crossed[l, g, :rows, :] = c.astype(BF)
            mid[l, image(g), :] = x_in + row("ls", l, 0) * c
        for at in blocks:
            v = mid[l, at, :] * row("scale", l, 1) + row("shift", l, 1)
            r["normed"][l, at, :] = v.astype(BF)
        weight_ready(0, l)
        for at in blocks:
            h = dot(r["normed"][l, at, :], weight(0, l), NN) + r["b1"][l]
            phi = 0.5 + 0.5 * lax.erf(h * SQRT_HALF)
            r["act"][l, at, :] = (h * phi).astype(BF)
            r["h"][l, at, :] = h.astype(BF)
            r["phi"][l, at, :] = phi.astype(BF)
        weight_ready(1, l)
        for at in blocks:
            branch = dot(r["act"][l, at, :], weight(1, l), NT) + r["b2"][l]
            r["branch"][l, at, :] = branch.astype(BF)
            x[l + 1, at, :] = mid[l, at, :] + row("ls", l, 1) * branch
    lax.fori_loop(0, layers, forward, None)
    for g in range(STEP):
        stage("tokf", g, x[layers, image(g), :])
        grad[image(g), :] = unstage("cotf", g)

    if not alone:

        @pl.when(step == 0)
        def _():
            pltpu.make_async_copy(r["carry"], gw, r["carried"]).wait()

    def backward(back, _):
        l = layers - 1 - back
        for at in blocks:
            g_out = grad[at, :]
            add(l, LS1, g_out * r["branch"][l, at, :].astype(F32))
            bg = row("ls", l, 1) * g_out
            add(l, B2, bg)
            r["bg"][at, :] = bg.astype(BF)
        for at in blocks:
            act_grad = dot(r["bg"][at, :], weight(1, l), NN)
            h = r["h"][l, at, :].astype(F32)
            slope = r["phi"][l, at, :].astype(F32) + h * (jnp.exp(h * h * -0.5) * PDF_SCALE)
            r["pg"][at, :] = (act_grad * slope).astype(BF)
        pg = r["pg"][:, columns]
        r["gb1"][l] += jnp.sum(pg.astype(F32).reshape(m // 8, 8, kept), axis=0)
        gw[0, l] += dot(r["normed"][l], pg, TN)
        gw[1, l] += dot(r["bg"][...], r["act"][l, :, columns], TN)
        for at in blocks:
            normed_grad = dot(r["pg"][at, :], weight(0, l), NT)
            add(l, S1, normed_grad * r["mid"][l, at, :])
            add(l, T1, normed_grad)
            grad[at, :] += row("scale", l, 1) * normed_grad
        for g in range(STEP):
            at = image(g)
            keep = r["keep"][g]
            mg = grad[at, :]
            add(l, LS0, mg * r["crossed"][l, g, :rows, :].astype(F32))
            cg = (row("ls", l, 0) * mg).astype(BF)
            r["gwc"][l] += dot(cg, r["mixed"][l, g], NT) * jnp.where(lane < patches, keep, 1.0)
            wk = r["wc"][l] * jnp.where(lane < patches, keep, 0.0).astype(BF)
            mixed_grad = dot(wk, cg, TN)[:rows]
            add(l, S0, mixed_grad * x[l, at, :])
            add(l, T0, mixed_grad)
            grad[at, :] = mg + row("scale", l, 0) * mixed_grad
    lax.fori_loop(0, layers, backward, None)
    for g in range(STEP):
        stage("cotf", g, grad[image(g), :])

    @pl.when(step == last)
    def _():
        def write_small(ref, wanted):
            for l in range(layers):
                sums = [jnp.sum(r["gsum"][l, k], axis=0, keepdims=True) for k in range(B1)]
                sums.append(jnp.sum(r["gb1"][l, :, wanted], axis=0, keepdims=True))
                table = jnp.concatenate(sums, axis=0)
                table = jnp.pad(table, ((0, 0), (0, 512 - sz.width)))
                gwc = jnp.pad(r["gwc"][l], ((0, 0), (0, 256 - depth)))
                full = jnp.concatenate([gwc, table[:, :256], table[:, 256:]], axis=0)
                ref[l] = full.astype(BF)

        for name, staged in (("out", "tokf"), ("tgrad", "cotf")):
            for c in range(sz.width // 128):
                v = r[staged][c, : patches * GROUP, :].reshape(patches, GROUP, 128)
                r[name][:, :, c * 128 : (c + 1) * 128] = v.astype(BF)

        def write_rows(ref, k, i, place, wanted):
            for l in range(layers):
                ref[k, l] = gw[i, l, place, wanted].astype(BF)

        if alone:
            write_small(r["small"], mine)
            write_small(r["send"], theirs)
            for i in range(2):
                for l in range(layers):
                    r["own"][i, l] = gw[i, l, :, mine]
                for k in range(sz.n_dp if sz.blocks else 1):
                    size = sz.shard if sz.blocks else sz.width
                    write_rows(r[f"blocks{i}"], k, i, slice(k * size, (k + 1) * size), theirs)
        else:
            write_small(r["small"], slice(None))
            for i in range(2):
                if sz.blocks:
                    for k in range(sz.n_dp):
                        at = meta[4 + (2 + i) * sz.n_dp + k] * sz.shard
                        at = pl.ds(pl.multiple_of(at, 16), sz.shard)
                        write_rows(r[f"blocks{i}"], k, i, at, slice(None))
                else:
                    write_rows(r[f"blocks{i}"], 0, i, slice(None), slice(None))


def run(sz, alone, meta, common, weights, carry=None):
    steps = GROUP // STEP
    w, m, layers = sz.width, sz.m, sz.layers
    kept = 2 * sz.own if alone else sz.own
    vmem = pl.BlockSpec(memory_space=pltpu.VMEM)
    anywhere = pl.BlockSpec(memory_space=pl.ANY)
    images = (sz.patches, GROUP, w)

    def group_spec(where):
        return pl.BlockSpec(
            images, lambda i, meta: (0, where(meta), 0), pipeline_mode=pl.Buffered(1)
        )

    def fixed_spec(block):
        return pl.BlockSpec(
            block, lambda i, meta: (0,) * len(block), pipeline_mode=pl.Buffered(1)
        )

    def in_all(meta):
        return meta[0]

    def in_part(meta):
        return 0

    keep_spec = pl.BlockSpec((STEP, 1, sz.depth), lambda i, meta: (meta[0] * steps + i, 0, 0))
    ins = [
        ("tok", common["tok"], group_spec(in_all)),
        ("cot", common["cot"], group_spec(in_all)),
        ("keep", common["keep"], keep_spec),
    ]
    for name in ("scale", "shift", "ls", "wc", "b1", "b2"):
        ins.append((name, common[name], vmem))
    scratch = []
    if sz.blocks:
        for l in range(layers):
            for i in range(2):
                for half in range(2):
                    ins.append((f"w{i}part{half}_{l}", weights[l][i][half], anywhere))
        scratch.append(("w", pltpu.VMEM((2, layers, w, sz.hidden), BF)))
        scratch.append(("arrive", pltpu.SemaphoreType.DMA((2, layers))))
    else:
        ins.append(("w", weights, vmem))
    if not alone:
        ins.append(("carry", carry, anywhere))
        scratch.append(("carried", pltpu.SemaphoreType.DMA))

    where, count = (in_part, GROUP) if alone else (in_all, sz.count)
    outs = [
        ("out", (sz.patches, count, w), BF, group_spec(where)),
        ("tgrad", (sz.patches, count, w), BF, group_spec(where)),
    ]
    small = (layers, sz.small, 256)
    block = (sz.n_dp, layers, sz.shard, sz.own) if sz.blocks else (1, layers, w, sz.own)
    outs.append(("small", small, BF, fixed_spec(small)))
    outs.append(("blocks0", block, BF, fixed_spec(block)))
    outs.append(("blocks1", block, BF, fixed_spec(block)))
    if alone:
        outs.append(("send", small, BF, fixed_spec(small)))
        own = (2, layers, w, sz.own)
        outs.append(("own", own, F32, fixed_spec(own)))
    for name, shape, dtype in (
        ("x", (layers + 1, m, w), F32),
        ("mid", (layers, m, w), F32),
        ("crossed", (layers, STEP, sz.depth, w), BF),
        ("mixed", (layers, STEP, sz.depth, w), BF),
        ("normed", (layers, m, w), BF),
        ("h", (layers, m, sz.hidden), BF),
        ("phi", (layers, m, sz.hidden), BF),
        ("act", (layers, m, sz.hidden), BF),
        ("branch", (layers, m, w), BF),
        ("grad", (m, w), F32),
        ("bg", (m, w), BF),
        ("pg", (m, sz.hidden), BF),
        ("gw", (2, layers, w, kept), F32),
        ("gwc", (layers, sz.rows, sz.depth), F32),
        ("gsum", (layers, B1, 8, w), F32),
        ("gb1", (layers, 8, kept), F32),
        ("tokf", (w // 128, GROUP * sz.rows, 128), F32),
        ("cotf", (w // 128, GROUP * sz.rows, 128), F32),
    ):
        scratch.append((name, pltpu.VMEM(shape, dtype)))
    names = ("meta",) + tuple(e[0] for e in ins + outs + scratch)
    flops = steps * m * 24 * w * sz.hidden
    results = pl.pallas_call(
        functools.partial(kernel_body, sz, kept, names),
        grid_spec=pltpu.PrefetchScalarGridSpec(
            num_scalar_prefetch=1,
            grid=(steps,),
            in_specs=[e[2] for e in ins],
            out_specs=[e[3] for e in outs],
            scratch_shapes=[e[1] for e in scratch],
        ),
        out_shape=[jax.ShapeDtypeStruct(e[1], e[2]) for e in outs],
        compiler_params=pltpu.CompilerParams(vmem_limit_bytes=60 * 2**20),
        cost_estimate=pl.CostEstimate(flops=flops, bytes_accessed=flops // 400, transcendentals=0),
    )(meta, *[e[1] for e in ins])
    return {e[0]: value for e, value in zip(outs, results)}


def swap(x, axis, k):
    n = lax.axis_size(axis)
    return lax.ppermute(x, axis, [(i, i ^ k) for i in range(n)])


def powers(n):
    return [2**k for k in range(1, n.bit_length() - 1)]


def gather_weights(sz, w1, w2):
    both = jnp.stack([w1, w2])
    parts = [both] + [swap(both, "hid", k) for k in range(1, sz.n_hid)]
    hid = lax.axis_index("hid")
    columns = []
    for j in range(sz.n_hid):
        v = parts[j]
        for h in range(1, sz.n_hid):
            v = jnp.where(hid == h, parts[j ^ h], v)
        columns.append(v)
    full = jnp.concatenate(columns, axis=2)
    got = [full[i][None] for i in range(2)]
    bits = powers(sz.n_dp)
    for step in range(len(bits)):
        moved = [swap(got[0], "dp", bits[step]), swap(got[1], "dp", bits[-1 - step])]
        got = [jnp.concatenate([g, v]) for g, v in zip(got, moved)]
    other = [swap(g, "dp", 1) for g in got]
    orders = []
    for seq in (bits, bits[::-1]):
        order = [0]
        for b in seq:
            order += [o ^ b for o in order]
        orders.append(order + [o ^ 1 for o in order])
    return got, other, orders


def exchange_orders(n_dp):
    bits = powers(n_dp)
    result = []
    for seq in ([1] + bits, [1] + bits[::-1]):
        order = [0]
        for b in reversed(seq):
            order = order + [o ^ b for o in order]
        result.append((seq, order))
    return result


def scatter_step(blocks, bit):
    n = blocks.shape[0] // 2
    got = swap(blocks[n:].astype(BF), "dp", bit)
    return blocks[:n].astype(F32) + got.astype(F32)


def on_device(
    tokens,
    masks,
    cotangent,
    aff_scale,
    aff_shift,
    layer_scale,
    crosspatch_weight,
    cross_bias,
    fc1_weight,
    fc1_bias,
    fc2_weight,
    fc2_bias,
):
    n_dp, n_hid = lax.axis_size("dp"), lax.axis_size("hid")
    sz = Sizes(tokens, fc1_weight, n_dp, n_hid)
    layers, patches = sz.layers, sz.patches
    me, hid = lax.axis_index("dp"), lax.axis_index("hid")
    half = hid % 2

    weights = []
    for l in range(layers):
        got, other, orders = gather_weights(sz, fc1_weight[l], fc2_weight[l])
        if sz.blocks:
            weights.append([(got[i], other[i]) for i in range(2)])
        else:
            ready = []
            for i in range(2):
                w = jnp.concatenate([got[i], other[i]])
                at = jnp.zeros(n_dp, jnp.int32).at[jnp.array(orders[i])].set(jnp.arange(n_dp))
                w = w[at[jnp.arange(n_dp) ^ me]]
                ready.append(w.reshape(sz.width, sz.hidden))
            weights.append(jnp.stack(ready))
    if not sz.blocks:
        weights = jnp.stack(weights, axis=1)

    bias_hi = cross_bias.astype(BF)
    bias_lo = (cross_bias - bias_hi.astype(F32)).astype(BF)
    wc = jnp.concatenate([crosspatch_weight, bias_hi[:, :, None], bias_lo[:, :, None]], axis=2)
    wc = jnp.pad(wc, ((0, 0), (0, sz.rows - patches), (0, sz.depth - patches - 2)))
    keep = jnp.pad(masks.astype(F32)[:, None, :], ((0, 0), (0, 0), (0, sz.depth - patches)))
    common = {
        "tok": tokens.transpose(1, 0, 2),
        "cot": cotangent.transpose(1, 0, 2),
        "keep": keep,
        "scale": aff_scale,
        "shift": aff_shift,
        "ls": layer_scale,
        "wc": wc,
        "b1": fc1_bias[:, None, :],
        "b2": fc2_bias[:, None, :],
    }
    exchanges = exchange_orders(n_dp)
    places = [me ^ k for k in orders[0] + orders[1]]
    places += [me ^ k for k in exchanges[0][1] + exchanges[1][1]]

    def meta(first, column):
        return jnp.stack([first, column, half, 1 - half] + places).astype(jnp.int32)

    first = run(sz, True, meta(half, hid // 2), common, weights)
    sent_out = swap(first["out"], "hid", 1)
    sent_grad = swap(first["tgrad"], "hid", 1)
    sent_small = swap(first["send"], "hid", 1)

    def by_owner(blocks):
        if sz.blocks:
            return blocks
        return jnp.moveaxis(blocks.reshape(layers, n_dp, sz.shard, sz.own), 1, 0)

    theirs = jnp.stack([by_owner(first[f"blocks{i}"]) for i in range(2)], axis=1)
    theirs = lax.all_to_all(theirs, "dp", split_axis=0, concat_axis=0, tiled=True)
    theirs = theirs.astype(F32).sum(axis=0).astype(BF)

    rest = run(sz, False, meta(jnp.int32(2), hid), common, weights, first["own"])
    gw = [by_owner(rest[f"blocks{i}"]) for i in range(2)]
    theirs, gw, small_rest = lax.optimization_barrier((theirs, gw, rest["small"]))
    theirs = swap(theirs, "hid", 1)
    if not sz.blocks:
        gw = [gw[i][jnp.array(exchanges[i][1]) ^ me] for i in range(2)]
    alone_small = first["small"].astype(F32) + sent_small.astype(F32)
    small = (alone_small + small_rest.astype(F32)).astype(BF)
    small = [small[l] for l in range(layers)]
    for k in range(len(exchanges[0][0])):
        gw = [scatter_step(gw[i], exchanges[i][0][k]) for i in range(2)]
        for l in range(layers):
            other = swap(small[l].astype(BF), "dp", exchanges[l % 2][0][k])
            small[l] = small[l].astype(BF).astype(F32) + other.astype(F32)
        if k == 0:
            gw, small, sent_out, sent_grad = lax.optimization_barrier(
                (gw, small, sent_out, sent_grad)
            )
    gw = [gw[i][0] + theirs[i].astype(F32) for i in range(2)]
    small = jnp.stack(small)
    gwc = small[:, :patches, :patches]
    sums = jnp.concatenate(
        [small[:, sz.rows : sz.rows + 8], small[:, sz.rows + 8 :, : sz.width - 256]], axis=2
    )

    def put(all_images, mine, theirs):
        all_images = lax.dynamic_update_slice_in_dim(all_images, mine, half * GROUP, axis=1)
        all_images = lax.dynamic_update_slice_in_dim(
            all_images, theirs, (1 - half) * GROUP, axis=1
        )
        return all_images.transpose(1, 0, 2)

    return (
        put(rest["out"], first["out"], sent_out),
        put(rest["tgrad"], first["tgrad"], sent_grad),
        jnp.stack([sums[:, S0], sums[:, S1]], axis=1),
        jnp.stack([sums[:, T0], sums[:, T1]], axis=1),
        jnp.stack([sums[:, LS0], sums[:, LS1]], axis=1),
        gwc,
        small[:, :patches, patches],
        gw[0],
        sums[:, B1],
        gw[1],
        sums[:, B2],
    )


def solution(mesh):
    return jax.shard_map(
        on_device,
        mesh=mesh,
        in_specs=(
            P("dp", None, None),
            P("dp", None),
            P("dp", None, None),
            P(),
            P(),
            P(),
            P(),
            P(),
            P(None, "dp", "hid"),
            P(),
            P(None, "dp", "hid"),
            P(),
        ),
        out_specs=(
            P("dp", None, None),
            P("dp", None, None),
            P(),
            P(),
            P(),
            P(),
            P(),
            P(None, "dp", "hid"),
            P(None, "hid"),
            P(None, "dp", "hid"),
            P(),
        ),
        check_vma=False,
    )
```

```python
import functools

import jax
import jax.numpy as jnp
from jax import lax
from jax.experimental import pallas as pl
from jax.experimental.pallas import tpu as pltpu
from jax.sharding import PartitionSpec as P

BF = jnp.bfloat16
F32 = jnp.float32
NN = (((1,), (0,)), ((), ()))
NT = (((1,), (1,)), ((), ()))
TN = (((0,), (0,)), ((), ()))
SQRT_HALF = 0.7071067811865476
PDF_SCALE = 0.3989422804014327
HALF_LOG2E = -0.7213475204444817
S0, T0, S1, T1, LS0, LS1, B2, B1 = range(8)
STEP = 4
GROUP = 8


def dot(a, b, dims):
    return lax.dot_general(a, b, dims, preferred_element_type=F32)


def round_up(n, k):
    return (n + k - 1) // k * k


class Sizes:
    def __init__(self, tokens, fc1, n_dp, n_hid):
        self.count, self.patches, self.width = tokens.shape
        self.layers, self.shard, self.own = fc1.shape
        self.n_dp, self.n_hid = n_dp, n_hid
        self.hidden = self.own * n_hid
        self.rows = round_up(self.patches, 8)
        self.depth = round_up(self.patches + 2, 16)
        self.m = STEP * self.rows
        self.small = self.rows + 16
        self.blocks = self.shard % 16 == 0 and self.own % 128 == 0


def kernel_body(sz, kept, names, *args):
    r = dict(zip(names, args))
    meta = r["meta"]
    step = pl.program_id(0)
    last = pl.num_programs(0) - 1
    layers, rows, patches, depth, m = sz.layers, sz.rows, sz.patches, sz.depth, sz.m
    alone = kept != sz.own
    whole = patches // 16 * 16
    pair = 2 * rows
    blocks = [slice(i, min(i + pair, m)) for i in range(0, m, pair)]
    lane = lax.broadcasted_iota(jnp.int32, (1, depth), 1)
    columns = pl.ds(pl.multiple_of(meta[1] * kept, 128), kept)
    mine = pl.ds(pl.multiple_of(meta[2] * sz.own, 128), sz.own)
    theirs = pl.ds(pl.multiple_of(meta[3] * sz.own, 128), sz.own)
    x, grad, gw = r["x"], r["grad"], r["gw"]

    group = pl.ds(pl.multiple_of(meta[0] * GROUP, GROUP), GROUP)
    buffers = {"tok": r["tokb"], "cot": r["cotb"]}

    cut = patches // 2
    results = (("out", "tok", 0, patches), ("tgrad", "cot", 0, cut), ("tgrad", "cot", cut, patches))

    def deliver(i):
        name, source, start, stop = results[i]
        place = r[f"{name}{i}"] if alone else r[name].at[start:stop, group, :]
        return pltpu.make_async_copy(buffers[source].at[start:stop], place, r["moved"].at[i])

    def bring(i):
        name, _, start, stop = results[i]
        place = r["pass_" + name].at[start:stop]
        return pltpu.make_async_copy(r[f"own_{name}{i}"], place, r["passed"].at[i])

    def pass_on(i):
        name, _, start, stop = results[i]
        at = pl.ds(pl.multiple_of(meta[2] * GROUP, GROUP), GROUP)
        source, place = r["pass_" + name].at[start:stop], r[name].at[start:stop, at, :]
        return pltpu.make_async_copy(source, place, r["passed"].at[i])

    def to_staging(name):
        staged = r[name + "f"]
        for c in range(sz.width // 128):
            part = r[name][:, :, c * 128 : (c + 1) * 128].astype(F32)
            staged[c, : patches * GROUP, :] = part.reshape(patches * GROUP, 128)
            staged[c, patches * GROUP :, :] = jnp.zeros(((rows - patches) * GROUP, 128), F32)

    def from_staging(name):
        for c in range(sz.width // 128):
            v = r[name + "f"][c, : patches * GROUP, :].reshape(patches, GROUP, 128)
            buffers[name][:, :, c * 128 : (c + 1) * 128] = v.astype(BF)

    @pl.when(step == 0)
    def _():
        if sz.blocks:
            for l in range(layers):
                for i in range(2):
                    for half in range(2):
                        src = r[f"w{i}part{half}_{l}"]
                        n_part = src.shape[0]
                        for k in range(n_part):
                            at = meta[4 + i * sz.n_dp + half * n_part + k] * sz.shard
                            at = pl.ds(pl.multiple_of(at, 16), sz.shard)
                            pltpu.make_async_copy(
                                src.at[k], r["w"].at[i, l, at], r["arrive"].at[i, l]
                            ).start()
        if not alone:
            pltpu.make_async_copy(r["carry"], gw, r["carried"]).start()
            for i in range(3):
                bring(i).start()
        for name in ("gwc", "gsum", "gb1") + (("gw",) if alone else ()):
            r[name][...] = jnp.zeros_like(r[name])
        to_staging("tok")
        to_staging("cot")
        for l in range(layers):
            r["b1s"][l] = r["b1"][l : l + 1, :]
            r["b2s"][l] = r["b2"][l : l + 1, :]

    def weight_ready(i, l):
        if sz.blocks:

            @pl.when(step == 0)
            def _():
                ref = r["w"].at[i, l]
                pltpu.make_async_copy(ref, ref, r["arrive"].at[i, l]).wait()

    def weight(i, l):
        return r["w"][i, l]

    def row(name, l, k):
        return r[name][l, k : k + 1, :]

    def image(g):
        return slice(g * rows, (g + 1) * rows)

    def add(l, kind, v):
        r["gsum"][l, kind] += jnp.sum(v.reshape(v.shape[0] // 8, 8, v.shape[1]), axis=0)

    def unstage(name, g):
        at = pl.ds(step * STEP + g, rows, stride=GROUP)
        return jnp.concatenate([r[name][c, at, :] for c in range(sz.width // 128)], axis=1)

    def stage(name, g, v):
        at = pl.ds(step * STEP + g, rows, stride=GROUP)
        for c in range(sz.width // 128):
            r[name][c, at, :] = v[:, c * 128 : (c + 1) * 128]

    for g in range(STEP):
        x[0, image(g), :] = unstage("tokf", g)
    share = STEP // layers

    def rows_of(g):
        return pl.ds(pl.multiple_of(g * rows, 8), rows)

    def forward(l, _):
        for g in range(share):
            grad[rows_of(l * share + g), :] = unstage("cotf", l * share + g)
        mid, mixed, crossed = r["mid"], r["mixed"], r["crossed"]
        for g in range(STEP):
            x_in = x[l, image(g), :]
            v = x_in * row("scale", l, 0) + row("shift", l, 0)
            mixed[l, g, :whole, :] = v[:whole].astype(BF)
            left = lax.broadcasted_iota(jnp.int32, (rows - whole, 1), 0) + whole
            tail = jnp.where(left < patches, v[whole:], 1.0)
            if depth > rows:
                tail = jnp.concatenate([tail, jnp.ones((depth - rows, sz.width), F32)], axis=0)
            mixed[l, g, whole:, :] = tail.astype(BF)
            wk = r["wc"][l] * jnp.where(lane < patches, r["keep"][g], 1.0).astype(BF)
            c = dot(wk, mixed[l, g], NN)
            crossed[l, g, :rows, :] = c.astype(BF)
            mid[l, image(g), :] = x_in + row("ls", l, 0) * c
        for at in blocks:
            v = mid[l, at, :] * row("scale", l, 1) + row("shift", l, 1)
            r["normed"][l, at, :] = v.astype(BF)
        weight_ready(0, l)
        for at in blocks:
            h = dot(r["normed"][l, at, :], weight(0, l), NN) + r["b1s"][l]
            phi = 0.5 + 0.5 * lax.erf(h * SQRT_HALF)
            r["act"][l, at, :] = (h * phi).astype(BF)
            r["h"][l, at, :] = h.astype(BF)
            r["phi"][l, at, :] = phi.astype(BF)
        weight_ready(1, l)
        for at in blocks:
            branch = dot(r["act"][l, at, :], weight(1, l), NT) + r["b2s"][l]
            r["branch"][l, at, :] = branch.astype(BF)
            x[l + 1, at, :] = mid[l, at, :] + row("ls", l, 1) * branch
    lax.fori_loop(0, layers, forward, None)
    @pl.when(step == 0)
    def _():
        if not alone:
            pltpu.make_async_copy(r["carry"], gw, r["carried"]).wait()

    @pl.when(step == last)
    def _():
        if not alone:
            for i in range(3):
                bring(i).wait()
                pass_on(i).start()

    def backward(back, _):
        l = layers - 1 - back
        for g in range(share):
            stage("tokf", back * share + g, x[layers, rows_of(back * share + g), :])
        for at in blocks:
            g_out = grad[at, :]
            add(l, LS1, g_out * r["branch"][l, at, :].astype(F32))
            bg = row("ls", l, 1) * g_out
            add(l, B2, bg)
            r["bg"][at, :] = bg.astype(BF)
        for at in blocks:
            act_grad = dot(r["bg"][at, :], weight(1, l), NN)
            h = r["h"][l, at, :]
            density = jnp.exp2(h * h * BF(HALF_LOG2E)) * BF(PDF_SCALE)
            r["pg"][at, :] = act_grad.astype(BF) * (r["phi"][l, at, :] + h * density)
        pg = r["pg"][:, columns]
        r["gb1"][l] += jnp.sum(pg.astype(F32).reshape(m // 8, 8, kept), axis=0)
        gw[0, l] += dot(r["normed"][l], pg, TN)
        gw[1, l] += dot(r["bg"][...], r["act"][l, :, columns], TN)
        for at in blocks:
            normed_grad = dot(r["pg"][at, :], weight(0, l), NT)
            add(l, S1, normed_grad * r["mid"][l, at, :])
            add(l, T1, normed_grad)
            grad[at, :] += row("scale", l, 1) * normed_grad
        for g in range(STEP):
            at = image(g)
            keep = r["keep"][g]
            mg = grad[at, :]
            add(l, LS0, mg * r["crossed"][l, g, :rows, :].astype(F32))
            cg = (row("ls", l, 0) * mg).astype(BF)
            r["gwc"][l] += dot(cg, r["mixed"][l, g], NT) * jnp.where(lane < patches, keep, 1.0)
            wk = r["wc"][l] * jnp.where(lane < patches, keep, 0.0).astype(BF)
            mixed_grad = dot(wk, cg, TN)[:rows]
            add(l, S0, mixed_grad * x[l, at, :])
            add(l, T0, mixed_grad)
            grad[at, :] = mg + row("scale", l, 0) * mixed_grad
    lax.fori_loop(0, layers, backward, None)
    for g in range(STEP):
        stage("cotf", g, grad[image(g), :])

    @pl.when(step == last)
    def _():
        def write_small(ref, wanted):
            for l in range(layers):
                sums = [jnp.sum(r["gsum"][l, k], axis=0, keepdims=True) for k in range(B1)]
                sums.append(jnp.sum(r["gb1"][l, :, wanted], axis=0, keepdims=True))
                table = jnp.concatenate(sums, axis=0)
                table = jnp.pad(table, ((0, 0), (0, 512 - sz.width)))
                gwc = jnp.pad(r["gwc"][l], ((0, 0), (0, 256 - depth)))
                full = jnp.concatenate([gwc, table[:, :256], table[:, 256:]], axis=0)
                ref[l] = full.astype(BF)

        from_staging("tok")
        deliver(0).start()
        from_staging("cot")
        deliver(1).start()
        deliver(2).start()

        if alone:
            write_small(r["small"], mine)
            write_small(r["send"], theirs)
            for i in range(2):
                for l in range(layers):
                    r["own"][i, l] = gw[i, l, :, mine]
                    for k in range(sz.n_dp if sz.blocks else 1):
                        size = sz.shard if sz.blocks else sz.width
                        place = slice(k * size, (k + 1) * size)
                        r["blocks"][k, i, l] = gw[i, l, place, theirs].astype(BF)
        else:
            write_small(r["small"], slice(None))
            for i in range(2):
                if sz.blocks:
                    n = sz.n_dp // 2
                    for k in range(sz.n_dp):
                        at = meta[4 + (2 + i) * sz.n_dp + k] * sz.shard
                        at = pl.ds(pl.multiple_of(at, 16), sz.shard)
                        ref = r[f"stay{i}"] if k < n else r[f"leave{i}"]
                        for l in range(layers):
                            ref[k % n, l] = gw[i, l, at, :].astype(BF)
                else:
                    for l in range(layers):
                        r[f"stay{i}"][0, l] = gw[i, l].astype(BF)
            for i in range(3):
                pass_on(i).wait()
        for i in range(3):
            deliver(i).wait()


def run(sz, alone, meta, common, weights, first=None):
    steps = GROUP // STEP
    w, m, layers = sz.width, sz.m, sz.layers
    kept = 2 * sz.own if alone else sz.own
    vmem = pl.BlockSpec(memory_space=pltpu.VMEM)
    anywhere = pl.BlockSpec(memory_space=pl.ANY)
    images = (sz.patches, GROUP, w)

    group_spec = pl.BlockSpec(
        images, lambda i, meta: (0, meta[0], 0), pipeline_mode=pl.Buffered(1)
    )

    def fixed_spec(block):
        return pl.BlockSpec(
            block, lambda i, meta: (0,) * len(block), pipeline_mode=pl.Buffered(1)
        )

    keep_spec = pl.BlockSpec((STEP, 1, sz.depth), lambda i, meta: (meta[0] * steps + i, 0, 0))
    ins = [
        ("tok", common["tok"], group_spec),
        ("cot", common["cot"], group_spec),
        ("keep", common["keep"], keep_spec),
    ]
    for name in ("scale", "shift", "ls", "wc", "b1", "b2"):
        ins.append((name, common[name], vmem))
    scratch = []
    if sz.blocks:
        for l in range(layers):
            for i in range(2):
                for half in range(2):
                    ins.append((f"w{i}part{half}_{l}", weights[l][i][half], anywhere))
        scratch.append(("w", pltpu.VMEM((2, layers, w, sz.hidden), BF)))
        scratch.append(("arrive", pltpu.SemaphoreType.DMA((2, layers))))
    else:
        ins.append(("w", weights, vmem))
    if not alone:
        ins.append(("carry", first["own"], anywhere))
        for name in ("out0", "tgrad1", "tgrad2"):
            ins.append(("own_" + name, first[name], anywhere))
        scratch.append(("passed", pltpu.SemaphoreType.DMA((3,))))
        scratch.append(("pass_out", pltpu.VMEM(images, BF)))
        scratch.append(("pass_tgrad", pltpu.VMEM(images, BF)))
        scratch.append(("carried", pltpu.SemaphoreType.DMA))

    if alone:
        cut = sz.patches // 2
        parts = (("out0", sz.patches), ("tgrad1", cut), ("tgrad2", sz.patches - cut))
        outs = [(name, (n, GROUP, w), BF, anywhere) for name, n in parts]
    else:
        outs = [(name, (sz.patches, sz.count, w), BF, anywhere) for name in ("out", "tgrad")]
    small = (layers, sz.small, 256)
    block = (layers, sz.shard, sz.own) if sz.blocks else (layers, w, sz.own)
    n_blocks = sz.n_dp if sz.blocks else 1
    outs.append(("small", small, BF, fixed_spec(small)))
    if not alone:
        part = ((n_blocks + 1) // 2,) + block
        for name in ("stay0", "stay1") + (("leave0", "leave1") if sz.blocks else ()):
            outs.append((name, part, BF, fixed_spec(part)))
    else:
        outs.append(("blocks", (n_blocks, 2) + block, BF, fixed_spec((n_blocks, 2) + block)))
        outs.append(("send", small, BF, fixed_spec(small)))
        own = (2, layers, w, sz.own)
        outs.append(("own", own, F32, fixed_spec(own)))
    for name, shape, dtype in (
        ("x", (layers + 1, m, w), F32),
        ("mid", (layers, m, w), F32),
        ("crossed", (layers, STEP, sz.depth, w), BF),
        ("mixed", (layers, STEP, sz.depth, w), BF),
        ("normed", (layers, m, w), BF),
        ("h", (layers, m, sz.hidden), BF),
        ("phi", (layers, m, sz.hidden), BF),
        ("act", (layers, m, sz.hidden), BF),
        ("branch", (layers, m, w), BF),
        ("grad", (m, w), F32),
        ("bg", (m, w), BF),
        ("pg", (m, sz.hidden), BF),
        ("gw", (2, layers, w, kept), F32),
        ("gwc", (layers, sz.rows, sz.depth), F32),
        ("gsum", (layers, B1, 8, w), F32),
        ("gb1", (layers, 8, kept), F32),
        ("b1s", (layers, 1, sz.hidden), F32),
        ("b2s", (layers, 1, w), F32),
        ("tokb", images, BF),
        ("cotb", images, BF),
        ("tokf", (w // 128, GROUP * sz.rows, 128), F32),
        ("cotf", (w // 128, GROUP * sz.rows, 128), F32),
    ):
        scratch.append((name, pltpu.VMEM(shape, dtype)))
    scratch.append(("moved", pltpu.SemaphoreType.DMA((3,))))
    names = ("meta",) + tuple(e[0] for e in ins + outs + scratch)
    flops = steps * m * 24 * w * sz.hidden
    results = pl.pallas_call(
        functools.partial(kernel_body, sz, kept, names),
        grid_spec=pltpu.PrefetchScalarGridSpec(
            num_scalar_prefetch=1,
            grid=(steps,),
            in_specs=[e[2] for e in ins],
            out_specs=[e[3] for e in outs],
            scratch_shapes=[e[1] for e in scratch],
        ),
        out_shape=[jax.ShapeDtypeStruct(e[1], e[2]) for e in outs],
        compiler_params=pltpu.CompilerParams(vmem_limit_bytes=60 * 2**20),
        cost_estimate=pl.CostEstimate(flops=flops, bytes_accessed=flops // 400, transcendentals=0),
    )(meta, *[e[1] for e in ins])
    return {e[0]: value for e, value in zip(outs, results)}


def swap(x, axis, k):
    n = lax.axis_size(axis)
    return lax.ppermute(x, axis, [(i, i ^ k) for i in range(n)])


def powers(n):
    return [2**k for k in range(1, n.bit_length() - 1)]


def gather_columns(sz, w1, w2):
    both = jnp.stack([w1, w2])
    parts = [both] + [swap(both, "hid", k) for k in range(1, sz.n_hid)]
    hid = lax.axis_index("hid")
    columns = []
    for j in range(sz.n_hid):
        v = parts[j]
        for h in range(1, sz.n_hid):
            v = jnp.where(hid == h, parts[j ^ h], v)
        columns.append(v)
    return jnp.concatenate(columns, axis=2)


def gather_rows(sz, full):
    got = [full[i][None] for i in range(2)]
    bits = powers(sz.n_dp)
    for step in range(len(bits)):
        moved = [swap(got[0], "dp", bits[step]), swap(got[1], "dp", bits[-1 - step])]
        got = [jnp.concatenate([g, v]) for g, v in zip(got, moved)]
    other = [swap(g, "dp", 1) for g in got]
    orders = []
    for seq in (bits, bits[::-1]):
        order = [0]
        for b in seq:
            order += [o ^ b for o in order]
        orders.append(order + [o ^ 1 for o in order])
    return got, other, orders


def exchange_orders(n_dp):
    bits = powers(n_dp)
    result = []
    for seq in ([1] + bits, [1] + bits[::-1]):
        order = [0]
        for b in reversed(seq):
            order = order + [o ^ b for o in order]
        result.append((seq, order))
    return result


def scatter_step(stay, leave, bit):
    got = swap(leave, "dp", bit)
    return stay.astype(F32) + got.astype(F32)


def halves(blocks):
    n = blocks.shape[0] // 2
    return blocks[:n], blocks[n:].astype(BF)


def finish_body(sz, *refs):
    (meta, keep0, keep1, got0, got1, theirs, small, got_s0, got_s1) = refs[:9]
    sent = refs[9:12]
    (out, tgrad, scale, shift, ls, gwc, gb, w1, b1, w2, b2, pass0, pass1, pass2, moved) = refs[14:]
    place = pl.ds(pl.multiple_of(meta[0] * GROUP, GROUP), GROUP)
    cut = sz.patches // 2
    spots = (out.at[:, place, :], tgrad.at[:cut, place, :], tgrad.at[cut:, place, :])
    brought, copies = [], []
    for i, buffer in enumerate((pass0, pass1, pass2)):
        brought.append(pltpu.make_async_copy(sent[i], buffer, moved.at[i]))
        copies.append(pltpu.make_async_copy(buffer, spots[i], moved.at[i]))
        brought[i].start()
    w1[...] = keep0[0] + got0[0].astype(F32) + theirs[0].astype(F32)
    w2[...] = keep1[0] + got1[0].astype(F32) + theirs[1].astype(F32)
    for i in range(3):
        brought[i].wait()
        copies[i].start()
    for l, got in enumerate((got_s0, got_s1)):
        total = small[l].astype(F32) + got[...].astype(F32)
        gwc[:, l, :] = total[: sz.patches, : sz.patches]
        lane = sz.patches // 128 * 128
        gb[l : l + 1, :] = total[:, lane : lane + 128].T[
            sz.patches - lane : sz.patches - lane + 1, : sz.patches
        ]
        low, high = total[sz.rows : sz.rows + 8], total[sz.rows + 8 : sz.rows + 16]
        table = jnp.concatenate([low, high[:, : sz.width - 256]], axis=1)
        for ref, kinds in ((scale, (S0, S1)), (shift, (T0, T1)), (ls, (LS0, LS1))):
            for k, kind in enumerate(kinds):
                ref[l, k : k + 1, :] = table[kind : kind + 1]
        b1[l : l + 1, :] = table[B1 : B1 + 1]
        b2[l : l + 1, :] = table[B2 : B2 + 1]
    for c in copies:
        c.wait()


def finish(sz, meta, keep, got, theirs, small, got_small, sent, out, tgrad):
    vmem = pl.BlockSpec(memory_space=pltpu.VMEM)
    anywhere = pl.BlockSpec(memory_space=pl.ANY)
    layers, w, p = sz.layers, sz.width, sz.patches
    vec = (layers, 2, w)
    shapes = [vec, vec, vec, (p, layers, p), (layers, p)]
    shapes += [(layers, sz.shard, sz.own), (layers, sz.own)] + [
        (layers, sz.shard, sz.own),
        (layers, w),
    ]
    whole = jax.ShapeDtypeStruct(out.shape, BF)
    return pl.pallas_call(
        functools.partial(finish_body, sz),
        grid_spec=pltpu.PrefetchScalarGridSpec(
            num_scalar_prefetch=1,
            grid=(),
            in_specs=[vmem] * 8 + [anywhere] * 5,
            out_specs=[anywhere] * 2 + [vmem] * 9,
            scratch_shapes=[pltpu.VMEM(v.shape, BF) for v in sent]
            + [pltpu.SemaphoreType.DMA((3,))],
        ),
        out_shape=[whole, whole] + [jax.ShapeDtypeStruct(s, F32) for s in shapes],
        input_output_aliases={12: 0, 13: 1},
        compiler_params=pltpu.CompilerParams(vmem_limit_bytes=32 * 2**20),
    )(meta, *keep, *got, theirs, small, *got_small, *sent, out, tgrad)


def on_device(
    tokens,
    masks,
    cotangent,
    aff_scale,
    aff_shift,
    layer_scale,
    crosspatch_weight,
    cross_bias,
    fc1_weight,
    fc1_bias,
    fc2_weight,
    fc2_bias,
):
    n_dp, n_hid = lax.axis_size("dp"), lax.axis_size("hid")
    sz = Sizes(tokens, fc1_weight, n_dp, n_hid)
    layers, patches = sz.layers, sz.patches
    me, hid = lax.axis_index("dp"), lax.axis_index("hid")
    half = hid % 2

    bias_hi = cross_bias.astype(BF)
    bias_lo = (cross_bias - bias_hi.astype(F32)).astype(BF)
    wc = jnp.concatenate([crosspatch_weight, bias_hi[:, :, None], bias_lo[:, :, None]], axis=2)
    wc = jnp.pad(wc, ((0, 0), (0, sz.rows - patches), (0, sz.depth - patches - 2)))
    keep = jnp.pad(masks.astype(F32)[:, None, :], ((0, 0), (0, 0), (0, sz.depth - patches)))

    weights = []
    for l in range(layers):
        full = gather_columns(sz, fc1_weight[l], fc2_weight[l])
        if l == 0:
            full, wc, keep = lax.optimization_barrier((full, wc, keep))
        got, other, orders = gather_rows(sz, full)
        if sz.blocks:
            weights.append([(got[i], other[i]) for i in range(2)])
        else:
            ready = []
            for i in range(2):
                w = jnp.concatenate([got[i], other[i]])
                at = jnp.zeros(n_dp, jnp.int32).at[jnp.array(orders[i])].set(jnp.arange(n_dp))
                w = w[at[jnp.arange(n_dp) ^ me]]
                ready.append(w.reshape(sz.width, sz.hidden))
            weights.append(jnp.stack(ready))
    if not sz.blocks:
        weights = jnp.stack(weights, axis=1)

    common = {
        "tok": tokens.transpose(1, 0, 2),
        "cot": cotangent.transpose(1, 0, 2),
        "keep": keep,
        "scale": aff_scale,
        "shift": aff_shift,
        "ls": layer_scale,
        "wc": wc,
        "b1": fc1_bias,
        "b2": fc2_bias,
    }
    exchanges = exchange_orders(n_dp)
    places = [me ^ k for k in orders[0] + orders[1]]
    places += [me ^ k for k in exchanges[0][1] + exchanges[1][1]]

    def meta(first, column):
        return jnp.stack([first, column, half, 1 - half] + places).astype(jnp.int32)

    first = run(sz, True, meta(half, hid // 2), common, weights)
    sent = [swap(first[name], "hid", 1) for name in ("out0", "tgrad1", "tgrad2")]
    sent_small = swap(first["send"], "hid", 1)

    theirs = first["blocks"]
    if not sz.blocks:
        theirs = theirs.reshape(2, layers, n_dp, sz.shard, sz.own)
        theirs = jnp.moveaxis(theirs, 2, 0)
    theirs = lax.all_to_all(theirs, "dp", split_axis=0, concat_axis=0, tiled=True)

    rest = run(sz, False, meta(jnp.int32(2), hid), common, weights, first)
    small_rest = rest["small"]
    if sz.blocks:
        gw = [(rest[f"stay{i}"], rest[f"leave{i}"]) for i in range(2)]
    else:
        gw = [rest[f"stay{i}"].reshape(layers, n_dp, sz.shard, sz.own) for i in range(2)]
        gw = [jnp.moveaxis(g, 1, 0)[jnp.array(e[1]) ^ me] for g, e in zip(gw, exchanges)]
        gw = [halves(g) for g in gw]
    gw, theirs, sent[:2] = lax.optimization_barrier((gw, theirs, sent[:2]))
    alone_small = first["small"].astype(F32) + sent_small.astype(F32)
    small = (alone_small + small_rest.astype(F32)).astype(BF)
    small = [small[l] for l in range(layers)]
    phases = len(exchanges[0][0])
    for k in range(phases - 1):
        gw = [scatter_step(*gw[i], exchanges[i][0][k]) for i in range(2)]
        for l in range(layers):
            other = swap(small[l], "dp", exchanges[l % 2][0][k])
            small[l] = (small[l].astype(F32) + other.astype(F32)).astype(BF)
        if k == 0:
            theirs = swap(theirs.astype(F32).sum(axis=0).astype(BF), "hid", 1)
        gw = [halves(g) for g in gw]
    got = [swap(gw[i][1], "dp", exchanges[i][0][-1]) for i in range(2)]
    got_small = [swap(small[l], "dp", exchanges[l % 2][0][-1]) for l in range(layers)]
    out, tgrad, scale, shift, ls, gwc, gb, w1, b1, w2, b2 = finish(
        sz,
        jnp.stack([1 - half]).astype(jnp.int32),
        [g[0] for g in gw],
        got,
        theirs,
        jnp.stack(small),
        got_small,
        sent,
        rest["out"],
        rest["tgrad"],
    )
    return (
        out.transpose(1, 0, 2),
        tgrad.transpose(1, 0, 2),
        scale,
        shift,
        ls,
        gwc.transpose(1, 0, 2),
        gb,
        w1,
        b1,
        w2,
        b2,
    )


def solution(mesh):
    return jax.shard_map(
        on_device,
        mesh=mesh,
        in_specs=(
            P("dp", None, None),
            P("dp", None),
            P("dp", None, None),
            P(),
            P(),
            P(),
            P(),
            P(),
            P(None, "dp", "hid"),
            P(),
            P(None, "dp", "hid"),
            P(),
        ),
        out_specs=(
            P("dp", None, None),
            P("dp", None, None),
            P(),
            P(),
            P(),
            P(),
            P(),
            P(None, "dp", "hid"),
            P(None, "hid"),
            P(None, "dp", "hid"),
            P(),
        ),
        check_vma=False,
    )
```

```python
import functools

import jax
import jax.numpy as jnp
from jax import lax
from jax.experimental import pallas as pl
from jax.experimental.pallas import tpu as pltpu
from jax.sharding import PartitionSpec as P

BF = jnp.bfloat16
F32 = jnp.float32
NN = (((1,), (0,)), ((), ()))
NT = (((1,), (1,)), ((), ()))
TN = (((0,), (0,)), ((), ()))
SQRT_HALF = 0.7071067811865476
PDF_SCALE = 0.3989422804014327
HALF_LOG2E = -0.7213475204444817
S0, T0, S1, T1, LS0, LS1, B2, B1 = range(8)
STEP = 4
GROUP = 8


def dot(a, b, dims):
    return lax.dot_general(a, b, dims, preferred_element_type=F32)


def round_up(n, k):
    return (n + k - 1) // k * k


class Sizes:
    def __init__(self, tokens, fc1, n_dp, n_hid):
        self.count, self.patches, self.width = tokens.shape
        self.layers, self.shard, self.own = fc1.shape
        self.n_dp, self.n_hid = n_dp, n_hid
        self.hidden = self.own * n_hid
        self.rows = round_up(self.patches, 8)
        self.depth = round_up(self.patches + 2, 16)
        self.m = STEP * self.rows
        self.tall = round_up(-(-2 * self.rows // 3), 8)
        self.small = self.tall + 8
        self.slot = self.layers * self.shard
        self.blocks = self.shard % 16 == 0 and self.own % 128 == 0


def sent_spots(sz):
    p, cut = sz.patches, sz.patches // 2
    return ((0, 0, p), (0, p, p + cut), (1, 0, p - cut))


def first_group(alone, meta):
    return meta[0] if alone else 2


def kernel_body(sz, kept, names, *args):
    r = dict(zip(names, args))
    meta = r["meta"]
    step = pl.program_id(0)
    last = pl.num_programs(0) - 1
    layers, rows, patches, depth, m = sz.layers, sz.rows, sz.patches, sz.depth, sz.m
    alone = kept != sz.own
    whole = patches // 16 * 16
    pair = 2 * rows
    blocks = [slice(i, min(i + pair, m)) for i in range(0, m, pair)]
    lane = lax.broadcasted_iota(jnp.int32, (1, depth), 1)
    columns = pl.ds(pl.multiple_of(meta[1 if alone else 2] * kept, 128), kept)
    mine = pl.ds(pl.multiple_of(meta[0] * sz.own, 128), sz.own)
    theirs = pl.ds(pl.multiple_of(meta[3] * sz.own, 128), sz.own)
    x, grad, gw = r["x"], r["grad"], r["gw"]

    group = pl.ds(pl.multiple_of(first_group(alone, meta) * GROUP, GROUP), GROUP)
    buffers = {"tok": r["tokb"], "cot": r["cotb"]}

    cut = patches // 2
    results = (("out", "tok", 0, patches), ("tgrad", "cot", 0, cut), ("tgrad", "cot", cut, patches))
    spots = sent_spots(sz)

    def deliver(i):
        name, source, start, stop = results[i]
        if alone:
            place = r[f"sent{spots[i][0]}"].at[spots[i][1] : spots[i][2]]
        else:
            place = r[name].at[start:stop, group, :]
        return pltpu.make_async_copy(buffers[source].at[start:stop], place, r["moved"].at[i])

    def bring(i):
        name, _, start, stop = results[i]
        place = r["pass_" + name].at[start:stop]
        source = r[f"own{spots[i][0]}"].at[spots[i][1] : spots[i][2]]
        return pltpu.make_async_copy(source, place, r["passed"].at[i])

    def pass_on(i):
        name, _, start, stop = results[i]
        at = pl.ds(pl.multiple_of(meta[0] * GROUP, GROUP), GROUP)
        source, place = r["pass_" + name].at[start:stop], r[name].at[start:stop, at, :]
        return pltpu.make_async_copy(source, place, r["passed"].at[i])

    def to_staging(name):
        staged = r[name + "f"]
        for c in range(sz.width // 128):
            part = r[name][:, :, c * 128 : (c + 1) * 128].astype(F32)
            staged[c, : patches * GROUP, :] = part.reshape(patches * GROUP, 128)
            staged[c, patches * GROUP :, :] = jnp.zeros(((rows - patches) * GROUP, 128), F32)

    def from_staging(name):
        for c in range(sz.width // 128):
            v = r[name + "f"][c, : patches * GROUP, :].reshape(patches, GROUP, 128)
            buffers[name][:, :, c * 128 : (c + 1) * 128] = v.astype(BF)

    @pl.when(step == 0)
    def _():
        if sz.blocks:
            for l in range(layers):
                for i in range(2):
                    for half in range(2):
                        src = r[f"w{i}part{half}_{l}"]
                        n_part = src.shape[0]
                        for k in range(n_part):
                            at = meta[4 + i * sz.n_dp + half * n_part + k] * sz.shard
                            at = pl.ds(pl.multiple_of(at, 16), sz.shard)
                            pltpu.make_async_copy(
                                src.at[k], r["w"].at[i, l, at], r["arrive"].at[i, l]
                            ).start()
        if not alone:
            pltpu.make_async_copy(r["carry"], gw, r["carried"]).start()
            for i in range(3):
                bring(i).start()
        for name in ("gwc", "gsum", "gb1") + (("gw",) if alone else ()):
            r[name][...] = jnp.zeros_like(r[name])
        r["keep"][...] = jnp.zeros_like(r["keep"])
        first_image = first_group(alone, meta) * GROUP
        for g in range(GROUP):
            r["keep"][g, :, :patches] = r["masks"][pl.ds(first_image + g, 1), :].astype(F32)
        wc = r["wc"]
        wc[...] = jnp.zeros_like(wc)
        r["bias"][...] = jnp.zeros_like(r["bias"])
        for l in range(layers):
            r["bias"][:, :patches] = jnp.broadcast_to(r["cb"][l : l + 1, :], (128, patches))
            column = r["bias"][...].T[:rows, : depth - 128]
            high = column.astype(BF)
            low = (column - high.astype(F32)).astype(BF)
            wc[l, :patches, :patches] = r["cw"][l]
            at = lane[:, 128:]
            extra = jnp.where(at == patches, high, jnp.where(at == patches + 1, low, 0.0))
            wc[l, :, 128:] = wc[l, :, 128:] + extra.astype(BF)
        to_staging("tok")
        to_staging("cot")
        for l in range(layers):
            r["b1s"][l] = r["b1"][l : l + 1, :]
            r["b2s"][l] = r["b2"][l : l + 1, :]

    def weight_ready(i, l):
        if sz.blocks:

            @pl.when(step == 0)
            def _():
                ref = r["w"].at[i, l]
                pltpu.make_async_copy(ref, ref, r["arrive"].at[i, l]).wait()

    def weight(i, l):
        return r["w"][i, l]

    def keep_of(g):
        return r["keep"][step * STEP + g]

    def row(name, l, k):
        return r[name][l, k : k + 1, :]

    def image(g):
        return slice(g * rows, (g + 1) * rows)

    def add(l, kind, v):
        r["gsum"][l, kind] += jnp.sum(v.reshape(v.shape[0] // 8, 8, v.shape[1]), axis=0)

    def unstage(name, g):
        at = pl.ds(step * STEP + g, rows, stride=GROUP)
        return jnp.concatenate([r[name][c, at, :] for c in range(sz.width // 128)], axis=1)

    def stage(name, g, v):
        at = pl.ds(step * STEP + g, rows, stride=GROUP)
        for c in range(sz.width // 128):
            r[name][c, at, :] = v[:, c * 128 : (c + 1) * 128]

    for g in range(STEP):
        x[0, image(g), :] = unstage("tokf", g)
    share = STEP // layers

    def rows_of(g):
        return pl.ds(pl.multiple_of(g * rows, 8), rows)

    def forward(l, _):
        for g in range(share):
            grad[rows_of(l * share + g), :] = unstage("cotf", l * share + g)
        mid, mixed, crossed = r["mid"], r["mixed"], r["crossed"]
        for g in range(STEP):
            x_in = x[l, image(g), :]
            v = x_in * row("scale", l, 0) + row("shift", l, 0)
            mixed[l, g, :whole, :] = v[:whole].astype(BF)
            left = lax.broadcasted_iota(jnp.int32, (rows - whole, 1), 0) + whole
            tail = jnp.where(left < patches, v[whole:], 1.0)
            if depth > rows:
                tail = jnp.concatenate([tail, jnp.ones((depth - rows, sz.width), F32)], axis=0)
            mixed[l, g, whole:, :] = tail.astype(BF)
            wk = r["wc"][l] * jnp.where(lane < patches, keep_of(g), 1.0).astype(BF)
            c = dot(wk, mixed[l, g], NN)
            crossed[l, g, :rows, :] = c.astype(BF)
            mid[l, image(g), :] = x_in + row("ls", l, 0) * c
        for at in blocks:
            v = mid[l, at, :] * row("scale", l, 1) + row("shift", l, 1)
            r["normed"][l, at, :] = v.astype(BF)
        weight_ready(0, l)
        for at in blocks:
            h = dot(r["normed"][l, at, :], weight(0, l), NN) + r["b1s"][l]
            phi = 0.5 + 0.5 * lax.erf(h * SQRT_HALF)
            r["act"][l, at, :] = (h * phi).astype(BF)
            r["h"][l, at, :] = h.astype(BF)
            r["phi"][l, at, :] = phi.astype(BF)
        weight_ready(1, l)
        for at in blocks:
            branch = dot(r["act"][l, at, :], weight(1, l), NT) + r["b2s"][l]
            r["branch"][l, at, :] = branch.astype(BF)
            x[l + 1, at, :] = mid[l, at, :] + row("ls", l, 1) * branch
    lax.fori_loop(0, layers, forward, None)
    @pl.when(step == 0)
    def _():
        if not alone:
            pltpu.make_async_copy(r["carry"], gw, r["carried"]).wait()

    @pl.when(step == last)
    def _():
        if not alone:
            for i in range(3):
                bring(i).wait()
                pass_on(i).start()

    def backward(back, _):
        l = layers - 1 - back
        for g in range(share):
            stage("tokf", back * share + g, x[layers, rows_of(back * share + g), :])
        for at in blocks:
            g_out = grad[at, :]
            add(l, LS1, g_out * r["branch"][l, at, :].astype(F32))
            bg = row("ls", l, 1) * g_out
            add(l, B2, bg)
            r["bg"][at, :] = bg.astype(BF)
        for at in blocks:
            act_grad = dot(r["bg"][at, :], weight(1, l), NN)
            h = r["h"][l, at, :]
            density = jnp.exp2(h * h * BF(HALF_LOG2E)) * BF(PDF_SCALE)
            r["pg"][at, :] = act_grad.astype(BF) * (r["phi"][l, at, :] + h * density)
        pg = r["pg"][:, columns]
        r["gb1"][l] += jnp.sum(pg.astype(F32).reshape(m // 8, 8, kept), axis=0)
        gw[0, l] += dot(r["normed"][l], pg, TN)
        gw[1, l] += dot(r["bg"][...], r["act"][l, :, columns], TN)
        for at in blocks:
            normed_grad = dot(r["pg"][at, :], weight(0, l), NT)
            add(l, S1, normed_grad * r["mid"][l, at, :])
            add(l, T1, normed_grad)
            grad[at, :] += row("scale", l, 1) * normed_grad
        for g in range(STEP):
            at = image(g)
            keep = keep_of(g)
            mg = grad[at, :]
            add(l, LS0, mg * r["crossed"][l, g, :rows, :].astype(F32))
            cg = (row("ls", l, 0) * mg).astype(BF)
            r["gwc"][l] += dot(cg, r["mixed"][l, g], NT) * jnp.where(lane < patches, keep, 1.0)
            wk = r["wc"][l] * jnp.where(lane < patches, keep, 0.0).astype(BF)
            mixed_grad = dot(wk, cg, TN)[:rows]
            add(l, S0, mixed_grad * x[l, at, :])
            add(l, T0, mixed_grad)
            grad[at, :] = mg + row("scale", l, 0) * mixed_grad
    lax.fori_loop(0, layers, backward, None)
    for g in range(STEP):
        stage("cotf", g, grad[image(g), :])

    @pl.when(step == last)
    def _():
        def write_small(ref, wanted):
            for l in range(layers):
                sums = [jnp.sum(r["gsum"][l, k], axis=0, keepdims=True) for k in range(B1)]
                sums.append(jnp.sum(r["gb1"][l, :, wanted], axis=0, keepdims=True))
                table = jnp.concatenate(sums, axis=0)
                low = r["gwc"][l, :, :128]
                high = jnp.pad(r["gwc"][l, :, 128:], ((0, 0), (0, 256 - depth)))
                a, b = sz.tall, 2 * sz.tall - rows
                last_part = jnp.pad(high[b:], ((0, 3 * a - 2 * rows), (0, 0)))
                middle = jnp.concatenate([low[a:], high[:b]], axis=0)
                wide = jnp.concatenate([low[:a], middle, last_part], axis=1)
                full = jnp.concatenate([wide, table], axis=0)
                if ref.shape[1] == 8:
                    n = sz.small // 8
                    full = full.reshape(n, 8, sz.width)
                    ref[l * n : (l + 1) * n] = full.astype(BF)
                else:
                    ref[l] = full.astype(BF)

        from_staging("tok")
        deliver(0).start()
        from_staging("cot")
        deliver(1).start()
        deliver(2).start()

        if alone:
            write_small(r["small"], mine)
            write_small(r["sends"], theirs)
            tail = spots[1][2]
            pltpu.make_async_copy(r["sends"], r["sent0"].at[tail:], r["moved"].at[3]).start()
            for i in range(2):
                for l in range(layers):
                    r["own"][i, l] = gw[i, l, :, mine]
                    for k in range(sz.n_dp if sz.blocks else 1):
                        size = sz.shard if sz.blocks else sz.width
                        place = slice(k * size, (k + 1) * size)
                        r["blocks"][k, i, l] = gw[i, l, place, theirs].astype(BF)
        else:
            write_small(r["small"], slice(None))
            for i in range(2):
                if sz.blocks:
                    n = sz.n_dp // 2
                    for k in range(sz.n_dp):
                        at = meta[4 + (2 + i) * sz.n_dp + k] * sz.shard
                        at = pl.ds(pl.multiple_of(at, 16), sz.shard)
                        ref = r[f"stay{i}"] if k < n else r[f"leave{i}"]
                        for l in range(layers):
                            to = (k % n) * sz.slot + l * sz.shard
                            ref[to : to + sz.shard, :] = gw[i, l, at, :].astype(BF)
                else:
                    for l in range(layers):
                        r[f"stay{i}"][l * sz.width : (l + 1) * sz.width, :] = gw[i, l].astype(BF)
            for i in range(3):
                pass_on(i).wait()
        for i in range(3):
            deliver(i).wait()
        if alone:
            tail = spots[1][2]
            pltpu.make_async_copy(r["sends"], r["sent0"].at[tail:], r["moved"].at[3]).wait()


def run(sz, alone, meta, common, weights, first=None):
    steps = GROUP // STEP
    w, m, layers = sz.width, sz.m, sz.layers
    kept = 2 * sz.own if alone else sz.own
    vmem = pl.BlockSpec(memory_space=pltpu.VMEM)
    anywhere = pl.BlockSpec(memory_space=pl.ANY)
    images = (sz.patches, GROUP, w)

    group_spec = pl.BlockSpec(
        images, lambda i, meta: (0, first_group(alone, meta), 0), pipeline_mode=pl.Buffered(1)
    )

    def fixed_spec(block):
        return pl.BlockSpec(
            block, lambda i, meta: (0,) * len(block), pipeline_mode=pl.Buffered(1)
        )

    ins = [
        ("tok", common["tok"], group_spec),
        ("cot", common["cot"], group_spec),
    ]
    for name in ("masks", "scale", "shift", "ls", "cw", "cb", "b1", "b2"):
        ins.append((name, common[name], vmem))
    scratch = []
    if sz.blocks:
        for l in range(layers):
            for i in range(2):
                for half in range(2):
                    ins.append((f"w{i}part{half}_{l}", weights[l][i][half], anywhere))
        scratch.append(("w", pltpu.VMEM((2, layers, w, sz.hidden), BF)))
        scratch.append(("arrive", pltpu.SemaphoreType.DMA((2, layers))))
    else:
        ins.append(("w", weights, vmem))
    if not alone:
        ins.append(("carry", first["own"], anywhere))
        for i in range(2):
            ins.append((f"own{i}", first[f"sent{i}"], anywhere))
        scratch.append(("passed", pltpu.SemaphoreType.DMA((3,))))
        scratch.append(("pass_out", pltpu.VMEM(images, BF)))
        scratch.append(("pass_tgrad", pltpu.VMEM(images, BF)))
        scratch.append(("carried", pltpu.SemaphoreType.DMA))

    if alone:
        spots, packed = sent_spots(sz), layers * sz.small // GROUP
        parts = (("sent0", spots[1][2] + packed), ("sent1", spots[2][2]))
        outs = [(name, (n, GROUP, w), BF, anywhere) for name, n in parts]
        scratch.append(("sends", pltpu.VMEM((packed, GROUP, w), BF)))
    else:
        outs = [(name, (sz.patches, sz.count, w), BF, anywhere) for name in ("out", "tgrad")]
    small = (layers, sz.small, w)
    block = (layers, sz.shard, sz.own) if sz.blocks else (layers, w, sz.own)
    n_blocks = sz.n_dp if sz.blocks else 1
    outs.append(("small", small, BF, fixed_spec(small)))
    if not alone:
        part = ((n_blocks + 1) // 2 * block[0] * block[1], sz.own)
        for name in ("stay0", "stay1") + (("leave0", "leave1") if sz.blocks else ()):
            outs.append((name, part, BF, fixed_spec(part)))
    else:
        outs.append(("blocks", (n_blocks, 2) + block, BF, fixed_spec((n_blocks, 2) + block)))
        own = (2, layers, w, sz.own)
        outs.append(("own", own, F32, fixed_spec(own)))
    for name, shape, dtype in (
        ("x", (layers + 1, m, w), F32),
        ("mid", (layers, m, w), F32),
        ("crossed", (layers, STEP, sz.depth, w), BF),
        ("mixed", (layers, STEP, sz.depth, w), BF),
        ("normed", (layers, m, w), BF),
        ("h", (layers, m, sz.hidden), BF),
        ("phi", (layers, m, sz.hidden), BF),
        ("act", (layers, m, sz.hidden), BF),
        ("branch", (layers, m, w), BF),
        ("grad", (m, w), F32),
        ("bg", (m, w), BF),
        ("pg", (m, sz.hidden), BF),
        ("gw", (2, layers, w, kept), F32),
        ("gwc", (layers, sz.rows, sz.depth), F32),
        ("gsum", (layers, B1, 8, w), F32),
        ("gb1", (layers, 8, kept), F32),
        ("keep", (GROUP, 1, sz.depth), F32),
        ("wc", (layers, sz.rows, sz.depth), BF),
        ("bias", (128, 256), F32),
        ("b1s", (layers, 1, sz.hidden), F32),
        ("b2s", (layers, 1, w), F32),
        ("tokb", images, BF),
        ("cotb", images, BF),
        ("tokf", (w // 128, GROUP * sz.rows, 128), F32),
        ("cotf", (w // 128, GROUP * sz.rows, 128), F32),
    ):
        scratch.append((name, pltpu.VMEM(shape, dtype)))
    scratch.append(("moved", pltpu.SemaphoreType.DMA((4,))))
    names = ("meta",) + tuple(e[0] for e in ins + outs + scratch)
    flops = steps * m * 24 * w * sz.hidden
    results = pl.pallas_call(
        functools.partial(kernel_body, sz, kept, names),
        grid_spec=pltpu.PrefetchScalarGridSpec(
            num_scalar_prefetch=1,
            grid=(steps,),
            in_specs=[e[2] for e in ins],
            out_specs=[e[3] for e in outs],
            scratch_shapes=[e[1] for e in scratch],
        ),
        out_shape=[jax.ShapeDtypeStruct(e[1], e[2]) for e in outs],
        compiler_params=pltpu.CompilerParams(vmem_limit_bytes=60 * 2**20),
        cost_estimate=pl.CostEstimate(flops=flops, bytes_accessed=flops // 400, transcendentals=0),
    )(meta, *[e[1] for e in ins])
    return {e[0]: value for e, value in zip(outs, results)}


def swap(x, axis, k):
    n = lax.axis_size(axis)
    return lax.ppermute(x, axis, [(i, i ^ k) for i in range(n)])


def powers(n):
    return [2**k for k in range(1, n.bit_length() - 1)]


def gather_columns(sz, w1, w2):
    both = jnp.stack([w1, w2])
    parts = [both] + [swap(both, "hid", k) for k in range(1, sz.n_hid)]
    hid = lax.axis_index("hid")
    columns = []
    for j in range(sz.n_hid):
        v = parts[j]
        for h in range(1, sz.n_hid):
            v = jnp.where(hid == h, parts[j ^ h], v)
        columns.append(v)
    return jnp.concatenate(columns, axis=2)


def gather_rows(sz, full):
    got = [full[i][None] for i in range(2)]
    bits = powers(sz.n_dp)
    for step in range(len(bits)):
        moved = [swap(got[0], "dp", bits[step]), swap(got[1], "dp", bits[-1 - step])]
        got = [jnp.concatenate([g, v]) for g, v in zip(got, moved)]
    return got


def gather_orders(n_dp):
    bits, orders = powers(n_dp), []
    for seq in (bits, bits[::-1]):
        order = [0]
        for b in seq:
            order += [o ^ b for o in order]
        orders.append(order + [o ^ 1 for o in order])
    return orders


def exchange_orders(n_dp):
    bits = powers(n_dp)
    result = []
    for seq in ([1] + bits, [1] + bits[::-1]):
        order = [0]
        for b in reversed(seq):
            order = order + [o ^ b for o in order]
        result.append((seq, order))
    return result


def place_body(sz, meta, sent0, sent1, _, __, out, tgrad, pass0, pass1, pass2, moved):
    place = pl.ds(pl.multiple_of(meta[3] * GROUP, GROUP), GROUP)
    cut = sz.patches // 2
    to = (out.at[:, place, :], tgrad.at[:cut, place, :], tgrad.at[cut:, place, :])
    brought, copies = [], []
    for i, buffer in enumerate((pass0, pass1, pass2)):
        which, start, stop = sent_spots(sz)[i]
        source = (sent0, sent1)[which].at[start:stop]
        brought.append(pltpu.make_async_copy(source, buffer, moved.at[i]))
        copies.append(pltpu.make_async_copy(buffer, to[i], moved.at[i]))
        brought[i].start()
    for i in range(3):
        brought[i].wait()
        copies[i].start()
    for c in copies:
        c.wait()


def place_images(sz, meta, sent, out, tgrad):
    anywhere = pl.BlockSpec(memory_space=pl.ANY)
    whole = jax.ShapeDtypeStruct(out.shape, BF)
    buffers = [(stop - start, GROUP, sz.width) for _, start, stop in sent_spots(sz)]
    return pl.pallas_call(
        functools.partial(place_body, sz),
        grid_spec=pltpu.PrefetchScalarGridSpec(
            num_scalar_prefetch=1,
            grid=(),
            in_specs=[anywhere] * 4,
            out_specs=[anywhere] * 2,
            scratch_shapes=[pltpu.VMEM(shape, BF) for shape in buffers]
            + [pltpu.SemaphoreType.DMA((3,))],
        ),
        out_shape=[whole, whole],
        input_output_aliases={3: 0, 4: 1},
        compiler_params=pltpu.CompilerParams(vmem_limit_bytes=16 * 2**20),
        cost_estimate=pl.CostEstimate(
            flops=0, bytes_accessed=8 * out.size // 3, transcendentals=0
        ),
    )(meta, *sent, out, tgrad)


def phase_body(sz, n, *refs):
    stays, gots, smalls, got_smalls = refs[:2], refs[2:4], refs[4:6], refs[6:8]
    keeps, pays = refs[8:10], refs[10:12]
    cut = n // 2 * sz.slot
    for i in range(2):
        total = stays[i][: n * sz.slot].astype(F32) + gots[i][: n * sz.slot].astype(F32)
        keeps[i][...] = total[:cut]
        pays[i][: n * sz.slot - cut] = total[cut:].astype(BF)
        own = smalls[i][smalls[i].shape[0] - sz.small :].astype(F32)
        other = got_smalls[i][got_smalls[i].shape[0] - sz.small :].astype(F32)
        pays[i][n * sz.slot - cut :] = (own + other).astype(BF)


def first_phase_body(sz, n, *refs):
    small, got_small, parts, total = refs[4], refs[5], refs[6], refs[11]
    smalls, got_smalls = ([v.at[i] for i in range(2)] for v in (small, got_small))
    phase_body(sz, n, *refs[:4], *smalls, *got_smalls, *refs[7:11])
    for i in range(2):
        v = parts[0, i].astype(F32)
        for k in range(1, sz.n_dp):
            v = v + parts[k, i].astype(F32)
        total[i] = v.astype(BF).reshape(sz.slot, sz.own)


def first_phase(sz, n, stays, gots, small, got_small, parts):
    if sz.blocks:
        cut = n // 2 * sz.slot
        keep = jax.ShapeDtypeStruct((cut, sz.own), F32)
        pay = jax.ShapeDtypeStruct((n * sz.slot - cut + sz.small, sz.own), BF)
        total = jax.ShapeDtypeStruct((2, sz.slot, sz.own), BF)
        out = pl.pallas_call(
            functools.partial(first_phase_body, sz, n),
            in_specs=[pl.BlockSpec(memory_space=pltpu.VMEM)] * 7,
            out_specs=[pl.BlockSpec(memory_space=pltpu.VMEM)] * 5,
            out_shape=[keep, keep, pay, pay, total],
            compiler_params=pltpu.CompilerParams(vmem_limit_bytes=32 * 2**20),
        )(*stays, *gots, small, got_small, parts)
        return out[:2], out[2:4], out[4]
    keeps, pays = phase(sz, n, stays, gots, small, got_small)
    return keeps, pays, parts.astype(F32).sum(axis=0).astype(BF).reshape(2, sz.slot, sz.own)


def phase(sz, n, stays, gots, smalls, got_smalls):
    if sz.blocks:
        cut = n // 2 * sz.slot
        keep = jax.ShapeDtypeStruct((cut, sz.own), F32)
        pay = jax.ShapeDtypeStruct((n * sz.slot - cut + sz.small, sz.own), BF)
        out = pl.pallas_call(
            functools.partial(phase_body, sz, n),
            in_specs=[pl.BlockSpec(memory_space=pltpu.VMEM)] * 8,
            out_specs=[pl.BlockSpec(memory_space=pltpu.VMEM)] * 4,
            out_shape=[keep, keep, pay, pay],
            compiler_params=pltpu.CompilerParams(vmem_limit_bytes=32 * 2**20),
        )(*stays, *gots, *smalls, *got_smalls)
        return out[:2], out[2:]
    keeps, pays = [], []
    for i in range(2):
        total = stays[i].astype(F32) + gots[i][: n * sz.slot].astype(F32)
        cut = n // 2 * sz.slot
        own, other = smalls[i][-sz.small :].astype(F32), got_smalls[i][-sz.small :].astype(F32)
        keeps.append(total[:cut])
        pays.append(jnp.concatenate([total[cut:], own + other]).astype(BF))
    return keeps, pays


def finish_body(sz, *refs):
    keeps, pays, gots, theirs = refs[0:2], refs[2:4], refs[4:6], refs[6]
    (scale, shift, ls, gwc, gb, w1, b1, w2, b2) = refs[7:]
    for i, ref in enumerate((w1, w2)):
        total = keeps[i][...] + gots[i][: keeps[i].shape[0]].astype(F32)
        ref[...] = total + theirs[i].astype(F32)
    for l in range(2):
        at = pays[l].shape[0] - sz.small
        total = pays[l][at:].astype(F32) + gots[l][at:].astype(F32)
        a, b = sz.tall, 2 * sz.tall - sz.rows
        low = jnp.concatenate([total[:a, :128], total[: sz.rows - a, 128:256]], axis=0)
        high = jnp.concatenate([total[sz.rows - a : a, 128:256], total[: sz.rows - b, 256:]], axis=0)
        gwc[:, l, :] = jnp.concatenate([low, high], axis=1)[: sz.patches, : sz.patches]
        lane = sz.patches - 128
        gb[l : l + 1, :] = high.T[lane : lane + 1, : sz.patches]
        table = total[a : a + 8]
        for ref, kinds in ((scale, (S0, S1)), (shift, (T0, T1)), (ls, (LS0, LS1))):
            for k, kind in enumerate(kinds):
                ref[l, k : k + 1, :] = table[kind : kind + 1]
        b1[l : l + 1, :] = table[B1 : B1 + 1]
        b2[l : l + 1, :] = table[B2 : B2 + 1]


def finish(sz, keeps, pays, gots, theirs):
    vmem = pl.BlockSpec(memory_space=pltpu.VMEM)
    layers, w, p = sz.layers, sz.width, sz.patches
    vec, rows = (layers, 2, w), (sz.slot, sz.own)
    if sz.slot % 16:
        gap = ((0, round_up(sz.slot, 16) - sz.slot), (0, 0))
        pays, gots = (
            [jnp.concatenate([jnp.pad(v[: sz.slot], gap), v[sz.slot :]]) for v in vs]
            for vs in (pays, gots)
        )
        keeps = [jnp.pad(v, gap) for v in keeps]
        theirs = jnp.pad(theirs, ((0, 0),) + gap)
        rows = (round_up(sz.slot, 16), sz.own)
    shapes = [vec, vec, vec, (p, layers, p), (layers, p), rows, (layers, sz.own), rows, (layers, w)]
    result = list(
        pl.pallas_call(
            functools.partial(finish_body, sz),
            in_specs=[vmem] * 7,
            out_specs=[vmem] * 9,
            out_shape=[jax.ShapeDtypeStruct(s, F32) for s in shapes],
            compiler_params=pltpu.CompilerParams(vmem_limit_bytes=32 * 2**20),
        )(*keeps, *pays, *gots, theirs)
    )
    for i in (5, 7):
        result[i] = result[i][: sz.slot].reshape(layers, sz.shard, sz.own)
    return result


def on_device(
    tokens,
    masks,
    cotangent,
    aff_scale,
    aff_shift,
    layer_scale,
    crosspatch_weight,
    cross_bias,
    fc1_weight,
    fc1_bias,
    fc2_weight,
    fc2_bias,
):
    n_dp, n_hid = lax.axis_size("dp"), lax.axis_size("hid")
    sz = Sizes(tokens, fc1_weight, n_dp, n_hid)
    layers, patches = sz.layers, sz.patches
    me, hid = lax.axis_index("dp"), lax.axis_index("hid")
    half = hid % 2

    orders, exchanges = gather_orders(n_dp), exchange_orders(n_dp)
    places = [half, hid // 2, hid, 1 - half] + [me ^ k for k in orders[0] + orders[1]]
    places += [me ^ k for k in exchanges[0][1] + exchanges[1][1]]
    meta = jnp.stack(places).astype(jnp.int32)

    weights = []
    for l in range(layers):
        got = gather_rows(sz, gather_columns(sz, fc1_weight[l], fc2_weight[l]))
        if l == 0:
            got, meta = lax.optimization_barrier((got, meta))
        other = [swap(g, "dp", 1) for g in got]
        if sz.blocks:
            weights.append([(got[i], other[i]) for i in range(2)])
        else:
            ready = []
            for i in range(2):
                w = jnp.concatenate([got[i], other[i]])
                at = jnp.zeros(n_dp, jnp.int32).at[jnp.array(orders[i])].set(jnp.arange(n_dp))
                w = w[at[jnp.arange(n_dp) ^ me]]
                ready.append(w.reshape(sz.width, sz.hidden))
            weights.append(jnp.stack(ready))
    if not sz.blocks:
        weights = jnp.stack(weights, axis=1)

    common = {
        "tok": tokens.transpose(1, 0, 2),
        "cot": cotangent.transpose(1, 0, 2),
        "masks": masks,
        "scale": aff_scale,
        "shift": aff_shift,
        "ls": layer_scale,
        "cw": crosspatch_weight,
        "cb": cross_bias,
        "b1": fc1_bias,
        "b2": fc2_bias,
    }
    first = run(sz, True, meta, common, weights)
    sent = [swap(first[f"sent{i}"], "hid", 1) for i in range(2)]

    theirs = first["blocks"]
    if not sz.blocks:
        theirs = theirs.reshape(2, layers, n_dp, sz.shard, sz.own)
        theirs = jnp.moveaxis(theirs, 2, 0)
    theirs = lax.all_to_all(theirs, "dp", split_axis=0, concat_axis=0, tiled=True)

    rest = run(sz, False, meta, common, weights, first)
    stays = [rest[f"stay{i}"] for i in range(2)]
    if sz.blocks:
        leaves = [rest[f"leave{i}"] for i in range(2)]
    else:
        whole = [g.reshape(layers, n_dp, sz.shard, sz.own) for g in stays]
        whole = [jnp.moveaxis(g, 1, 0)[jnp.array(e[1]) ^ me] for g, e in zip(whole, exchanges)]
        whole = [g.reshape(2, -1, sz.own) for g in whole]
        stays, leaves = [g[0] for g in whole], [g[1] for g in whole]
    leaves, theirs, sent[0] = lax.optimization_barrier((leaves, theirs, sent[0]))
    small = sent[0][sent_spots(sz)[1][2] :].reshape(layers, sz.small, sz.width)
    small = first["small"].astype(F32) + small.astype(F32)
    small = (small + rest["small"].astype(F32)).astype(BF)
    got_small = swap(small, "dp", 1)
    gots = [swap(v, "dp", 1) for v in leaves]
    n = n_dp // 2
    keeps, pays, theirs = first_phase(sz, n, stays, gots, small, got_small, theirs)
    theirs = swap(theirs, "hid", 1)
    for k in range(1, len(exchanges[0][0]) - 1):
        n //= 2
        gots = [swap(pays[i], "dp", exchanges[i][0][k]) for i in range(2)]
        keeps, pays = phase(sz, n, keeps, gots, pays, gots)
    gots = [swap(pays[i], "dp", exchanges[i][0][-1]) for i in range(2)]
    out, tgrad = place_images(sz, meta, sent, rest["out"], rest["tgrad"])
    scale, shift, ls, gwc, gb, w1, b1, w2, b2 = finish(sz, keeps, pays, gots, theirs)
    return (
        out.transpose(1, 0, 2),
        tgrad.transpose(1, 0, 2),
        scale,
        shift,
        ls,
        gwc.transpose(1, 0, 2),
        gb,
        w1,
        b1,
        w2,
        b2,
    )


def solution(mesh):
    return jax.shard_map(
        on_device,
        mesh=mesh,
        in_specs=(
            P("dp", None, None),
            P("dp", None),
            P("dp", None, None),
            P(),
            P(),
            P(),
            P(),
            P(),
            P(None, "dp", "hid"),
            P(),
            P(None, "dp", "hid"),
            P(),
        ),
        out_specs=(
            P("dp", None, None),
            P("dp", None, None),
            P(),
            P(),
            P(),
            P(),
            P(),
            P(None, "dp", "hid"),
            P(None, "hid"),
            P(None, "dp", "hid"),
            P(),
        ),
        check_vma=False,
    )
```

```python
import functools

import jax
import jax.numpy as jnp
from jax import lax
from jax.experimental import pallas as pl
from jax.experimental.pallas import tpu as pltpu
from jax.sharding import PartitionSpec as P

BF = jnp.bfloat16
F32 = jnp.float32
NN = (((1,), (0,)), ((), ()))
NT = (((1,), (1,)), ((), ()))
TN = (((0,), (0,)), ((), ()))
SQRT_HALF = 0.7071067811865476
PDF_SCALE = 0.3989422804014327
HALF_LOG2E = -0.7213475204444817
S0, T0, S1, T1, LS0, LS1, B2, B1 = range(8)
STEP = 4
GROUP = 8


def dot(a, b, dims):
    return lax.dot_general(a, b, dims, preferred_element_type=F32)


def round_up(n, k):
    return (n + k - 1) // k * k


class Sizes:
    def __init__(self, tokens, fc1, n_dp, n_hid):
        self.count, self.patches, self.width = tokens.shape
        self.layers, self.shard, self.own = fc1.shape
        self.n_dp, self.n_hid = n_dp, n_hid
        self.hidden = self.own * n_hid
        self.rows = round_up(self.patches, 8)
        self.depth = round_up(self.patches + 2, 16)
        self.m = STEP * self.rows
        self.tall = round_up(-(-2 * self.rows // 3), 8)
        self.small = self.tall + 8
        self.slot = self.layers * self.shard
        self.blocks = self.shard % 16 == 0 and self.own % 128 == 0


def sent_spots(sz):
    p, cut = sz.patches, sz.patches // 2
    return ((0, 0, p), (0, p, p + cut), (1, 0, p - cut))


def first_group(alone, meta):
    return meta[0] if alone else 2


def kernel_body(sz, kept, names, *args):
    r = dict(zip(names, args))
    meta = r["meta"]
    step = pl.program_id(0)
    last = pl.num_programs(0) - 1
    layers, rows, patches, depth, m = sz.layers, sz.rows, sz.patches, sz.depth, sz.m
    alone = kept != sz.own
    whole = patches // 16 * 16
    pair = 2 * rows
    blocks = [slice(i, min(i + pair, m)) for i in range(0, m, pair)]
    lane = lax.broadcasted_iota(jnp.int32, (1, depth), 1)
    columns = pl.ds(pl.multiple_of(meta[1 if alone else 2] * kept, 128), kept)
    mine = pl.ds(pl.multiple_of(meta[0] * sz.own, 128), sz.own)
    theirs = pl.ds(pl.multiple_of(meta[3] * sz.own, 128), sz.own)
    x, grad, gw = r["x"], r["grad"], r["gw"]

    group = pl.ds(pl.multiple_of(first_group(alone, meta) * GROUP, GROUP), GROUP)
    buffers = {"tok": r["tokb"], "cot": r["cotb"]}

    cut = patches // 2
    results = (("out", "tok", 0, patches), ("tgrad", "cot", 0, cut), ("tgrad", "cot", cut, patches))
    spots = sent_spots(sz)

    def deliver(i):
        name, source, start, stop = results[i]
        if alone:
            place = r[f"sent{spots[i][0]}"].at[spots[i][1] : spots[i][2]]
        else:
            place = r[name].at[start:stop, group, :]
        return pltpu.make_async_copy(buffers[source].at[start:stop], place, r["moved"].at[i])

    def bring(i):
        name, _, start, stop = results[i]
        place = r["pass_" + name].at[start:stop]
        source = r[f"own{spots[i][0]}"].at[spots[i][1] : spots[i][2]]
        return pltpu.make_async_copy(source, place, r["passed"].at[i])

    def pass_on(i):
        name, _, start, stop = results[i]
        at = pl.ds(pl.multiple_of(meta[0] * GROUP, GROUP), GROUP)
        source, place = r["pass_" + name].at[start:stop], r[name].at[start:stop, at, :]
        return pltpu.make_async_copy(source, place, r["passed"].at[i])

    def to_staging(name):
        staged = r[name + "f"]
        for c in range(sz.width // 128):
            part = r[name][:, :, c * 128 : (c + 1) * 128].astype(F32)
            staged[c, : patches * GROUP, :] = part.reshape(patches * GROUP, 128)
            staged[c, patches * GROUP :, :] = jnp.zeros(((rows - patches) * GROUP, 128), F32)

    def from_staging(name):
        for c in range(sz.width // 128):
            v = r[name + "f"][c, : patches * GROUP, :].reshape(patches, GROUP, 128)
            buffers[name][:, :, c * 128 : (c + 1) * 128] = v.astype(BF)

    @pl.when(step == 0)
    def _():
        if sz.blocks:
            for l in range(layers):
                for i in range(2):
                    for half in range(2):
                        src = r[f"w{i}part{half}_{l}"]
                        n_part = src.shape[0]
                        for k in range(n_part):
                            at = meta[4 + l * sz.n_dp + half * n_part + k] * sz.shard
                            at = pl.ds(pl.multiple_of(at, 16), sz.shard)
                            pltpu.make_async_copy(
                                src.at[k], r["w"].at[i, l, at], r["arrive"].at[i, l]
                            ).start()
        if not alone:
            pltpu.make_async_copy(r["carry"], gw, r["carried"]).start()
            for i in range(3):
                bring(i).start()
        for name in ("gwc", "gsum", "gb1") + (("gw",) if alone else ()):
            r[name][...] = jnp.zeros_like(r[name])
        r["keep"][...] = jnp.zeros_like(r["keep"])
        first_image = first_group(alone, meta) * GROUP
        for g in range(GROUP):
            r["keep"][g, :, :patches] = r["masks"][pl.ds(first_image + g, 1), :].astype(F32)
        wc = r["wc"]
        wc[...] = jnp.zeros_like(wc)
        r["bias"][...] = jnp.zeros_like(r["bias"])
        for l in range(layers):
            r["bias"][:, :patches] = jnp.broadcast_to(r["cb"][l : l + 1, :], (128, patches))
            column = r["bias"][...].T[:rows, : depth - 128]
            high = column.astype(BF)
            low = (column - high.astype(F32)).astype(BF)
            wc[l, :patches, :patches] = r["cw"][l]
            at = lane[:, 128:]
            extra = jnp.where(at == patches, high, jnp.where(at == patches + 1, low, 0.0))
            wc[l, :, 128:] = wc[l, :, 128:] + extra.astype(BF)
        to_staging("tok")
        to_staging("cot")
        for l in range(layers):
            r["b1s"][l] = r["b1"][l : l + 1, :]
            r["b2s"][l] = r["b2"][l : l + 1, :]

    def weight_ready(i, l):
        if sz.blocks:

            @pl.when(step == 0)
            def _():
                ref = r["w"].at[i, l]
                pltpu.make_async_copy(ref, ref, r["arrive"].at[i, l]).wait()

    def weight(i, l):
        return r["w"][i, l]

    def keep_of(g):
        return r["keep"][step * STEP + g]

    def row(name, l, k):
        return r[name][l, k : k + 1, :]

    def image(g):
        return slice(g * rows, (g + 1) * rows)

    def add(l, kind, v):
        r["gsum"][l, kind] += jnp.sum(v.reshape(v.shape[0] // 8, 8, v.shape[1]), axis=0)

    def unstage(name, g):
        at = pl.ds(step * STEP + g, rows, stride=GROUP)
        return jnp.concatenate([r[name][c, at, :] for c in range(sz.width // 128)], axis=1)

    def stage(name, g, v):
        at = pl.ds(step * STEP + g, rows, stride=GROUP)
        for c in range(sz.width // 128):
            r[name][c, at, :] = v[:, c * 128 : (c + 1) * 128]

    for g in range(STEP):
        x[0, image(g), :] = unstage("tokf", g)
    share = STEP // layers

    def rows_of(g):
        return pl.ds(pl.multiple_of(g * rows, 8), rows)

    def forward(l, _):
        for g in range(share):
            grad[rows_of(l * share + g), :] = unstage("cotf", l * share + g)
        mid, mixed, crossed = r["mid"], r["mixed"], r["crossed"]
        for g in range(STEP):
            x_in = x[l, image(g), :]
            v = x_in * row("scale", l, 0) + row("shift", l, 0)
            mixed[l, g, :whole, :] = v[:whole].astype(BF)
            left = lax.broadcasted_iota(jnp.int32, (rows - whole, 1), 0) + whole
            tail = jnp.where(left < patches, v[whole:], 1.0)
            if depth > rows:
                tail = jnp.concatenate([tail, jnp.ones((depth - rows, sz.width), F32)], axis=0)
            mixed[l, g, whole:, :] = tail.astype(BF)
            wk = r["wc"][l] * jnp.where(lane < patches, keep_of(g), 1.0).astype(BF)
            c = dot(wk, mixed[l, g], NN)
            crossed[l, g, :rows, :] = c.astype(BF)
            mid[l, image(g), :] = x_in + row("ls", l, 0) * c
        for at in blocks:
            v = mid[l, at, :] * row("scale", l, 1) + row("shift", l, 1)
            r["normed"][l, at, :] = v.astype(BF)
        weight_ready(0, l)
        for at in blocks:
            h = dot(r["normed"][l, at, :], weight(0, l), NN) + r["b1s"][l]
            phi = 0.5 + 0.5 * lax.erf(h * SQRT_HALF)
            r["act"][l, at, :] = (h * phi).astype(BF)
            r["h"][l, at, :] = h.astype(BF)
            r["phi"][l, at, :] = phi.astype(BF)
        weight_ready(1, l)
        for at in blocks:
            branch = dot(r["act"][l, at, :], weight(1, l), NT) + r["b2s"][l]
            r["branch"][l, at, :] = branch.astype(BF)
            x[l + 1, at, :] = mid[l, at, :] + row("ls", l, 1) * branch
    lax.fori_loop(0, layers, forward, None)
    @pl.when(step == 0)
    def _():
        if not alone:
            pltpu.make_async_copy(r["carry"], gw, r["carried"]).wait()

    @pl.when(step == last)
    def _():
        if not alone:
            for i in range(3):
                bring(i).wait()
                pass_on(i).start()

    def backward(back, _):
        l = layers - 1 - back
        for g in range(share):
            stage("tokf", back * share + g, x[layers, rows_of(back * share + g), :])
        for at in blocks:
            g_out = grad[at, :]
            add(l, LS1, g_out * r["branch"][l, at, :].astype(F32))
            bg = row("ls", l, 1) * g_out
            add(l, B2, bg)
            r["bg"][at, :] = bg.astype(BF)
        for at in blocks:
            act_grad = dot(r["bg"][at, :], weight(1, l), NN)
            h = r["h"][l, at, :]
            density = jnp.exp2(h * h * BF(HALF_LOG2E)) * BF(PDF_SCALE)
            r["pg"][at, :] = act_grad.astype(BF) * (r["phi"][l, at, :] + h * density)
        pg = r["pg"][:, columns]
        r["gb1"][l] += jnp.sum(pg.astype(F32).reshape(m // 8, 8, kept), axis=0)
        gw[0, l] += dot(r["normed"][l], pg, TN)
        gw[1, l] += dot(r["bg"][...], r["act"][l, :, columns], TN)
        for at in blocks:
            normed_grad = dot(r["pg"][at, :], weight(0, l), NT)
            add(l, S1, normed_grad * r["mid"][l, at, :])
            add(l, T1, normed_grad)
            grad[at, :] += row("scale", l, 1) * normed_grad
        for g in range(STEP):
            at = image(g)
            keep = keep_of(g)
            mg = grad[at, :]
            add(l, LS0, mg * r["crossed"][l, g, :rows, :].astype(F32))
            cg = (row("ls", l, 0) * mg).astype(BF)
            r["gwc"][l] += dot(cg, r["mixed"][l, g], NT) * jnp.where(lane < patches, keep, 1.0)
            wk = r["wc"][l] * jnp.where(lane < patches, keep, 0.0).astype(BF)
            mixed_grad = dot(wk, cg, TN)[:rows]
            add(l, S0, mixed_grad * x[l, at, :])
            add(l, T0, mixed_grad)
            grad[at, :] = mg + row("scale", l, 0) * mixed_grad
    lax.fori_loop(0, layers, backward, None)
    for g in range(STEP):
        stage("cotf", g, grad[image(g), :])

    @pl.when(step == last)
    def _():
        def write_small(ref, wanted):
            for l in range(layers):
                sums = [jnp.sum(r["gsum"][l, k], axis=0, keepdims=True) for k in range(B1)]
                sums.append(jnp.sum(r["gb1"][l, :, wanted], axis=0, keepdims=True))
                table = jnp.concatenate(sums, axis=0)
                low = r["gwc"][l, :, :128]
                high = jnp.pad(r["gwc"][l, :, 128:], ((0, 0), (0, 256 - depth)))
                a, b = sz.tall, 2 * sz.tall - rows
                last_part = jnp.pad(high[b:], ((0, 3 * a - 2 * rows), (0, 0)))
                middle = jnp.concatenate([low[a:], high[:b]], axis=0)
                wide = jnp.concatenate([low[:a], middle, last_part], axis=1)
                full = jnp.concatenate([wide, table], axis=0)
                if ref.shape[1] == 8:
                    n = sz.small // 8
                    full = full.reshape(n, 8, sz.width)
                    ref[l * n : (l + 1) * n] = full.astype(BF)
                else:
                    ref[l] = full.astype(BF)

        from_staging("tok")
        deliver(0).start()
        from_staging("cot")
        deliver(1).start()
        deliver(2).start()

        if alone:
            write_small(r["small"], mine)
            write_small(r["sends"], theirs)
            tail = spots[1][2]
            pltpu.make_async_copy(r["sends"], r["sent0"].at[tail:], r["moved"].at[3]).start()
            for i in range(2):
                for l in range(layers):
                    r["own"][i, l] = gw[i, l, :, mine]
                    for k in range(sz.n_dp if sz.blocks else 1):
                        size = sz.shard if sz.blocks else sz.width
                        place = slice(k * size, (k + 1) * size)
                        r["blocks"][k, i, l] = gw[i, l, place, theirs].astype(BF)
        else:
            write_small(r["small"], slice(None))
            for i in range(2):
                if sz.blocks:
                    n = sz.n_dp // 2
                    for k in range(sz.n_dp):
                        at = meta[4 + (2 + i) * sz.n_dp + k] * sz.shard
                        at = pl.ds(pl.multiple_of(at, 16), sz.shard)
                        ref = r[f"stay{i}"] if k < n else r[f"leave{i}"]
                        for l in range(layers):
                            to = (k % n) * sz.slot + l * sz.shard
                            ref[to : to + sz.shard, :] = gw[i, l, at, :].astype(BF)
                else:
                    for l in range(layers):
                        r[f"stay{i}"][l * sz.width : (l + 1) * sz.width, :] = gw[i, l].astype(BF)
            for i in range(3):
                pass_on(i).wait()
        for i in range(3):
            deliver(i).wait()
        if alone:
            tail = spots[1][2]
            pltpu.make_async_copy(r["sends"], r["sent0"].at[tail:], r["moved"].at[3]).wait()


def run(sz, alone, meta, common, weights, first=None):
    steps = GROUP // STEP
    w, m, layers = sz.width, sz.m, sz.layers
    kept = 2 * sz.own if alone else sz.own
    vmem = pl.BlockSpec(memory_space=pltpu.VMEM)
    anywhere = pl.BlockSpec(memory_space=pl.ANY)
    images = (sz.patches, GROUP, w)

    group_spec = pl.BlockSpec(
        images, lambda i, meta: (0, first_group(alone, meta), 0), pipeline_mode=pl.Buffered(1)
    )

    def fixed_spec(block):
        return pl.BlockSpec(
            block, lambda i, meta: (0,) * len(block), pipeline_mode=pl.Buffered(1)
        )

    ins = [
        ("tok", common["tok"], group_spec),
        ("cot", common["cot"], group_spec),
    ]
    for name in ("masks", "scale", "shift", "ls", "cw", "cb", "b1", "b2"):
        ins.append((name, common[name], vmem))
    scratch = []
    if sz.blocks:
        for l in range(layers):
            for i in range(2):
                for half in range(2):
                    ins.append((f"w{i}part{half}_{l}", weights[l][i][half], anywhere))
        scratch.append(("w", pltpu.VMEM((2, layers, w, sz.hidden), BF)))
        scratch.append(("arrive", pltpu.SemaphoreType.DMA((2, layers))))
    else:
        ins.append(("w", weights, vmem))
    if not alone:
        ins.append(("carry", first["own"], anywhere))
        for i in range(2):
            ins.append((f"own{i}", first[f"sent{i}"], anywhere))
        scratch.append(("passed", pltpu.SemaphoreType.DMA((3,))))
        scratch.append(("pass_out", pltpu.VMEM(images, BF)))
        scratch.append(("pass_tgrad", pltpu.VMEM(images, BF)))
        scratch.append(("carried", pltpu.SemaphoreType.DMA))

    if alone:
        spots, packed = sent_spots(sz), layers * sz.small // GROUP
        parts = (("sent0", spots[1][2] + packed), ("sent1", spots[2][2]))
        outs = [(name, (n, GROUP, w), BF, anywhere) for name, n in parts]
        scratch.append(("sends", pltpu.VMEM((packed, GROUP, w), BF)))
    else:
        outs = [(name, (sz.patches, sz.count, w), BF, anywhere) for name in ("out", "tgrad")]
    small = (layers, sz.small, w)
    block = (layers, sz.shard, sz.own) if sz.blocks else (layers, w, sz.own)
    n_blocks = sz.n_dp if sz.blocks else 1
    outs.append(("small", small, BF, fixed_spec(small)))
    if not alone:
        part = ((n_blocks + 1) // 2 * block[0] * block[1], sz.own)
        for name in ("stay0", "stay1") + (("leave0", "leave1") if sz.blocks else ()):
            outs.append((name, part, BF, fixed_spec(part)))
    else:
        outs.append(("blocks", (n_blocks, 2) + block, BF, fixed_spec((n_blocks, 2) + block)))
        own = (2, layers, w, sz.own)
        outs.append(("own", own, F32, fixed_spec(own)))
    for name, shape, dtype in (
        ("x", (layers + 1, m, w), F32),
        ("mid", (layers, m, w), F32),
        ("crossed", (layers, STEP, sz.depth, w), BF),
        ("mixed", (layers, STEP, sz.depth, w), BF),
        ("normed", (layers, m, w), BF),
        ("h", (layers, m, sz.hidden), BF),
        ("phi", (layers, m, sz.hidden), BF),
        ("act", (layers, m, sz.hidden), BF),
        ("branch", (layers, m, w), BF),
        ("grad", (m, w), F32),
        ("bg", (m, w), BF),
        ("pg", (m, sz.hidden), BF),
        ("gw", (2, layers, w, kept), F32),
        ("gwc", (layers, sz.rows, sz.depth), F32),
        ("gsum", (layers, B1, 8, w), F32),
        ("gb1", (layers, 8, kept), F32),
        ("keep", (GROUP, 1, sz.depth), F32),
        ("wc", (layers, sz.rows, sz.depth), BF),
        ("bias", (128, 256), F32),
        ("b1s", (layers, 1, sz.hidden), F32),
        ("b2s", (layers, 1, w), F32),
        ("tokb", images, BF),
        ("cotb", images, BF),
        ("tokf", (w // 128, GROUP * sz.rows, 128), F32),
        ("cotf", (w // 128, GROUP * sz.rows, 128), F32),
    ):
        scratch.append((name, pltpu.VMEM(shape, dtype)))
    scratch.append(("moved", pltpu.SemaphoreType.DMA((4,))))
    names = ("meta",) + tuple(e[0] for e in ins + outs + scratch)
    flops = steps * m * 24 * w * sz.hidden
    results = pl.pallas_call(
        functools.partial(kernel_body, sz, kept, names),
        grid_spec=pltpu.PrefetchScalarGridSpec(
            num_scalar_prefetch=1,
            grid=(steps,),
            in_specs=[e[2] for e in ins],
            out_specs=[e[3] for e in outs],
            scratch_shapes=[e[1] for e in scratch],
        ),
        out_shape=[jax.ShapeDtypeStruct(e[1], e[2]) for e in outs],
        compiler_params=pltpu.CompilerParams(vmem_limit_bytes=60 * 2**20),
        cost_estimate=pl.CostEstimate(flops=flops, bytes_accessed=flops // 400, transcendentals=0),
    )(meta, *[e[1] for e in ins])
    return {e[0]: value for e, value in zip(outs, results)}


def swap(x, axis, k):
    n = lax.axis_size(axis)
    return lax.ppermute(x, axis, [(i, i ^ k) for i in range(n)])


def powers(n):
    return [2**k for k in range(1, n.bit_length() - 1)]


def gather_columns(sz, both, later, hid):
    parts = [both] + [swap(both, "hid", k) for k in range(1, sz.n_hid)]
    if later is not None:
        parts[1:3], later = lax.optimization_barrier((parts[1:3], later))
    columns = []
    for j in range(sz.n_hid):
        v = parts[j]
        for h in range(1, sz.n_hid):
            v = jnp.where(hid == h, parts[j ^ h], v)
        columns.append(v)
    return jnp.concatenate(columns, axis=2), later


def gather_rows(sz, full):
    got = [full[i][None] for i in range(2)]
    bits = powers(sz.n_dp)
    for step in range(len(bits)):
        moved = [swap(got[0], "dp", bits[step]), swap(got[1], "dp", bits[-1 - step])]
        got = [jnp.concatenate([g, v]) for g, v in zip(got, moved)]
    return got


def gather_orders(n_dp):
    bits, orders = powers(n_dp), []
    for seq in (bits, bits[::-1]):
        order = [0]
        for b in seq:
            order += [o ^ b for o in order]
        orders.append(order + [o ^ 1 for o in order])
    return orders


def exchange_orders(n_dp):
    bits = powers(n_dp)
    result = []
    for seq in ([1] + bits, [1] + bits[::-1]):
        order = [0]
        for b in reversed(seq):
            order = order + [o ^ b for o in order]
        result.append((seq, order))
    return result


def place_body(sz, meta, sent0, sent1, _, __, out, tgrad, pass0, pass1, pass2, moved):
    place = pl.ds(pl.multiple_of(meta[3] * GROUP, GROUP), GROUP)
    cut = sz.patches // 2
    to = (out.at[:, place, :], tgrad.at[:cut, place, :], tgrad.at[cut:, place, :])
    brought, copies = [], []
    for i, buffer in enumerate((pass0, pass1, pass2)):
        which, start, stop = sent_spots(sz)[i]
        source = (sent0, sent1)[which].at[start:stop]
        brought.append(pltpu.make_async_copy(source, buffer, moved.at[i]))
        copies.append(pltpu.make_async_copy(buffer, to[i], moved.at[i]))
        brought[i].start()
    for i in range(3):
        brought[i].wait()
        copies[i].start()
    for c in copies:
        c.wait()


def place_images(sz, meta, sent, out, tgrad):
    anywhere = pl.BlockSpec(memory_space=pl.ANY)
    whole = jax.ShapeDtypeStruct(out.shape, BF)
    buffers = [(stop - start, GROUP, sz.width) for _, start, stop in sent_spots(sz)]
    return pl.pallas_call(
        functools.partial(place_body, sz),
        grid_spec=pltpu.PrefetchScalarGridSpec(
            num_scalar_prefetch=1,
            grid=(),
            in_specs=[anywhere] * 4,
            out_specs=[anywhere] * 2,
            scratch_shapes=[pltpu.VMEM(shape, BF) for shape in buffers]
            + [pltpu.SemaphoreType.DMA((3,))],
        ),
        out_shape=[whole, whole],
        input_output_aliases={3: 0, 4: 1},
        compiler_params=pltpu.CompilerParams(vmem_limit_bytes=16 * 2**20),
        cost_estimate=pl.CostEstimate(
            flops=0, bytes_accessed=8 * out.size // 3, transcendentals=0
        ),
    )(meta, *sent, out, tgrad)


def phase_body(sz, n, *refs):
    stays, gots, smalls, got_smalls = refs[:2], refs[2:4], refs[4:6], refs[6:8]
    keeps, pays = refs[8:10], refs[10:12]
    cut = n // 2 * sz.slot
    for i in range(2):
        total = stays[i][: n * sz.slot].astype(F32) + gots[i][: n * sz.slot].astype(F32)
        keeps[i][...] = total[:cut]
        pays[i][: n * sz.slot - cut] = total[cut:].astype(BF)
        own = smalls[i][smalls[i].shape[0] - sz.small :].astype(F32)
        other = got_smalls[i][got_smalls[i].shape[0] - sz.small :].astype(F32)
        pays[i][n * sz.slot - cut :] = (own + other).astype(BF)


def first_phase_body(sz, n, *refs):
    small, got_small, parts, total = refs[4], refs[5], refs[6], refs[11]
    smalls, got_smalls = ([v.at[i] for i in range(2)] for v in (small, got_small))
    phase_body(sz, n, *refs[:4], *smalls, *got_smalls, *refs[7:11])
    for i in range(2):
        v = parts[0, i].astype(F32)
        for k in range(1, sz.n_dp):
            v = v + parts[k, i].astype(F32)
        total[i] = v.astype(BF).reshape(sz.slot, sz.own)


def first_phase(sz, n, stays, gots, small, got_small, parts):
    if sz.blocks:
        cut = n // 2 * sz.slot
        keep = jax.ShapeDtypeStruct((cut, sz.own), F32)
        pay = jax.ShapeDtypeStruct((n * sz.slot - cut + sz.small, sz.own), BF)
        total = jax.ShapeDtypeStruct((2, sz.slot, sz.own), BF)
        out = pl.pallas_call(
            functools.partial(first_phase_body, sz, n),
            in_specs=[pl.BlockSpec(memory_space=pltpu.VMEM)] * 7,
            out_specs=[pl.BlockSpec(memory_space=pltpu.VMEM)] * 5,
            out_shape=[keep, keep, pay, pay, total],
            compiler_params=pltpu.CompilerParams(vmem_limit_bytes=32 * 2**20),
        )(*stays, *gots, small, got_small, parts)
        return out[:2], out[2:4], out[4]
    keeps, pays = phase(sz, n, stays, gots, small, got_small)
    return keeps, pays, parts.astype(F32).sum(axis=0).astype(BF).reshape(2, sz.slot, sz.own)


def phase(sz, n, stays, gots, smalls, got_smalls):
    if sz.blocks:
        cut = n // 2 * sz.slot
        keep = jax.ShapeDtypeStruct((cut, sz.own), F32)
        pay = jax.ShapeDtypeStruct((n * sz.slot - cut + sz.small, sz.own), BF)
        out = pl.pallas_call(
            functools.partial(phase_body, sz, n),
            in_specs=[pl.BlockSpec(memory_space=pltpu.VMEM)] * 8,
            out_specs=[pl.BlockSpec(memory_space=pltpu.VMEM)] * 4,
            out_shape=[keep, keep, pay, pay],
            compiler_params=pltpu.CompilerParams(vmem_limit_bytes=32 * 2**20),
        )(*stays, *gots, *smalls, *got_smalls)
        return out[:2], out[2:]
    keeps, pays = [], []
    for i in range(2):
        total = stays[i].astype(F32) + gots[i][: n * sz.slot].astype(F32)
        cut = n // 2 * sz.slot
        own, other = smalls[i][-sz.small :].astype(F32), got_smalls[i][-sz.small :].astype(F32)
        keeps.append(total[:cut])
        pays.append(jnp.concatenate([total[cut:], own + other]).astype(BF))
    return keeps, pays


def finish_body(sz, *refs):
    keeps, pays, gots, theirs = refs[0:2], refs[2:4], refs[4:6], refs[6]
    (scale, shift, ls, gwc, gb, w1, b1, w2, b2) = refs[7:]
    for i, ref in enumerate((w1, w2)):
        total = keeps[i][...] + gots[i][: keeps[i].shape[0]].astype(F32)
        ref[...] = total + theirs[i].astype(F32)
    for l in range(2):
        at = pays[l].shape[0] - sz.small
        total = pays[l][at:].astype(F32) + gots[l][at:].astype(F32)
        a, b = sz.tall, 2 * sz.tall - sz.rows
        low = jnp.concatenate([total[:a, :128], total[: sz.rows - a, 128:256]], axis=0)
        high = jnp.concatenate([total[sz.rows - a : a, 128:256], total[: sz.rows - b, 256:]], axis=0)
        gwc[:, l, :] = jnp.concatenate([low, high], axis=1)[: sz.patches, : sz.patches]
        lane = sz.patches - 128
        gb[l : l + 1, :] = high.T[lane : lane + 1, : sz.patches]
        table = total[a : a + 8]
        for ref, kinds in ((scale, (S0, S1)), (shift, (T0, T1)), (ls, (LS0, LS1))):
            for k, kind in enumerate(kinds):
                ref[l, k : k + 1, :] = table[kind : kind + 1]
        b1[l : l + 1, :] = table[B1 : B1 + 1]
        b2[l : l + 1, :] = table[B2 : B2 + 1]


def finish(sz, keeps, pays, gots, theirs):
    vmem = pl.BlockSpec(memory_space=pltpu.VMEM)
    layers, w, p = sz.layers, sz.width, sz.patches
    vec, rows = (layers, 2, w), (sz.slot, sz.own)
    if sz.slot % 16:
        gap = ((0, round_up(sz.slot, 16) - sz.slot), (0, 0))
        pays, gots = (
            [jnp.concatenate([jnp.pad(v[: sz.slot], gap), v[sz.slot :]]) for v in vs]
            for vs in (pays, gots)
        )
        keeps = [jnp.pad(v, gap) for v in keeps]
        theirs = jnp.pad(theirs, ((0, 0),) + gap)
        rows = (round_up(sz.slot, 16), sz.own)
    shapes = [vec, vec, vec, (p, layers, p), (layers, p), rows, (layers, sz.own), rows, (layers, w)]
    result = list(
        pl.pallas_call(
            functools.partial(finish_body, sz),
            in_specs=[vmem] * 7,
            out_specs=[vmem] * 9,
            out_shape=[jax.ShapeDtypeStruct(s, F32) for s in shapes],
            compiler_params=pltpu.CompilerParams(vmem_limit_bytes=32 * 2**20),
        )(*keeps, *pays, *gots, theirs)
    )
    for i in (5, 7):
        result[i] = result[i][: sz.slot].reshape(layers, sz.shard, sz.own)
    return result


def on_device(
    tokens,
    masks,
    cotangent,
    aff_scale,
    aff_shift,
    layer_scale,
    crosspatch_weight,
    cross_bias,
    fc1_weight,
    fc1_bias,
    fc2_weight,
    fc2_bias,
):
    n_dp, n_hid = lax.axis_size("dp"), lax.axis_size("hid")
    sz = Sizes(tokens, fc1_weight, n_dp, n_hid)
    layers, patches = sz.layers, sz.patches
    me, hid = lax.axis_index("dp"), lax.axis_index("hid")
    half = hid % 2

    orders, exchanges = gather_orders(n_dp), exchange_orders(n_dp)
    places = [half, hid // 2, hid, 1 - half] + [me ^ k for k in orders[0] + orders[1]]
    places += [me ^ k for k in exchanges[0][1] + exchanges[1][1]]
    meta = jnp.stack(places).astype(jnp.int32)

    weights = []
    gathered, later, chip = [], fc2_weight, hid
    for i in range(2):
        full, later = gather_columns(sz, later if i else fc1_weight, None if i else later, chip)
        full, chip = lax.optimization_barrier((full, chip))
        got = gather_rows(sz, full)
        if i == 0:
            got, meta = lax.optimization_barrier((got, meta))
        gathered.append((got, [swap(g, "dp", 1) for g in got]))
    for l in range(layers):
        got, other = ([gathered[i][part][l] for i in range(2)] for part in range(2))
        if sz.blocks:
            weights.append([(got[i], other[i]) for i in range(2)])
        else:
            ready = []
            for i in range(2):
                w = jnp.concatenate([got[i], other[i]])
                at = jnp.zeros(n_dp, jnp.int32).at[jnp.array(orders[l])].set(jnp.arange(n_dp))
                w = w[at[jnp.arange(n_dp) ^ me]]
                ready.append(w.reshape(sz.width, sz.hidden))
            weights.append(jnp.stack(ready))
    if not sz.blocks:
        weights = jnp.stack(weights, axis=1)

    common = {
        "tok": tokens.transpose(1, 0, 2),
        "cot": cotangent.transpose(1, 0, 2),
        "masks": masks,
        "scale": aff_scale,
        "shift": aff_shift,
        "ls": layer_scale,
        "cw": crosspatch_weight,
        "cb": cross_bias,
        "b1": fc1_bias,
        "b2": fc2_bias,
    }
    first = run(sz, True, meta, common, weights)
    sent = [swap(first[f"sent{i}"], "hid", 1) for i in range(2)]

    theirs = first["blocks"]
    if not sz.blocks:
        theirs = theirs.reshape(2, layers, n_dp, sz.shard, sz.own)
        theirs = jnp.moveaxis(theirs, 2, 0)
    theirs = lax.all_to_all(theirs, "dp", split_axis=0, concat_axis=0, tiled=True)

    rest = run(sz, False, meta, common, weights, first)
    stays = [rest[f"stay{i}"] for i in range(2)]
    if sz.blocks:
        leaves = [rest[f"leave{i}"] for i in range(2)]
    else:
        whole = [g.reshape(layers, n_dp, sz.shard, sz.own) for g in stays]
        whole = [jnp.moveaxis(g, 1, 0)[jnp.array(e[1]) ^ me] for g, e in zip(whole, exchanges)]
        whole = [g.reshape(2, -1, sz.own) for g in whole]
        stays, leaves = [g[0] for g in whole], [g[1] for g in whole]
    leaves, theirs, sent[0] = lax.optimization_barrier((leaves, theirs, sent[0]))
    small = sent[0][sent_spots(sz)[1][2] :].reshape(layers, sz.small, sz.width)
    small = first["small"].astype(F32) + small.astype(F32)
    small = (small + rest["small"].astype(F32)).astype(BF)
    got_small = swap(small, "dp", 1)
    gots = [swap(v, "dp", 1) for v in leaves]
    n = n_dp // 2
    keeps, pays, theirs = first_phase(sz, n, stays, gots, small, got_small, theirs)
    theirs = swap(theirs, "hid", 1)
    for k in range(1, len(exchanges[0][0]) - 1):
        n //= 2
        gots = [swap(pays[i], "dp", exchanges[i][0][k]) for i in range(2)]
        keeps, pays = phase(sz, n, keeps, gots, pays, gots)
    gots = [swap(pays[i], "dp", exchanges[i][0][-1]) for i in range(2)]
    out, tgrad = place_images(sz, meta, sent, rest["out"], rest["tgrad"])
    scale, shift, ls, gwc, gb, w1, b1, w2, b2 = finish(sz, keeps, pays, gots, theirs)
    return (
        out.transpose(1, 0, 2),
        tgrad.transpose(1, 0, 2),
        scale,
        shift,
        ls,
        gwc.transpose(1, 0, 2),
        gb,
        w1,
        b1,
        w2,
        b2,
    )


def solution(mesh):
    return jax.shard_map(
        on_device,
        mesh=mesh,
        in_specs=(
            P("dp", None, None),
            P("dp", None),
            P("dp", None, None),
            P(),
            P(),
            P(),
            P(),
            P(),
            P(None, "dp", "hid"),
            P(),
            P(None, "dp", "hid"),
            P(),
        ),
        out_specs=(
            P("dp", None, None),
            P("dp", None, None),
            P(),
            P(),
            P(),
            P(),
            P(),
            P(None, "dp", "hid"),
            P(None, "hid"),
            P(None, "dp", "hid"),
            P(),
        ),
        check_vma=False,
    )
```

```python
import functools

import jax
import jax.numpy as jnp
from jax import lax
from jax.experimental import pallas as pl
from jax.experimental.pallas import tpu as pltpu
from jax.sharding import PartitionSpec as P

BF = jnp.bfloat16
F32 = jnp.float32
NN = (((1,), (0,)), ((), ()))
NT = (((1,), (1,)), ((), ()))
TN = (((0,), (0,)), ((), ()))
SQRT_HALF = 0.7071067811865476
PDF_SCALE = 0.3989422804014327
HALF_LOG2E = -0.7213475204444817
S0, T0, S1, T1, LS0, LS1, B2, B1 = range(8)
STEP = 4
GROUP = 8


def dot(a, b, dims):
    return lax.dot_general(a, b, dims, preferred_element_type=F32)


def round_up(n, k):
    return (n + k - 1) // k * k


class Sizes:
    def __init__(self, tokens, fc1, n_dp, n_hid):
        self.count, self.patches, self.width = tokens.shape
        self.layers, self.shard, self.own = fc1.shape
        self.n_dp, self.n_hid = n_dp, n_hid
        self.hidden = self.own * n_hid
        self.rows = round_up(self.patches, 8)
        self.depth = round_up(self.patches + 2, 16)
        self.m = STEP * self.rows
        self.tall = round_up(-(-2 * self.rows // 3), 8)
        self.small = self.tall + 8
        self.slot = self.layers * self.shard
        self.blocks = self.shard % 16 == 0 and self.own % 128 == 0


def sent_spots(sz):
    p, cut = sz.patches, sz.patches // 2
    return ((0, 0, p), (0, p, p + cut), (1, 0, p - cut))


def first_group(alone, meta):
    return meta[0] if alone else 2


def kernel_body(sz, kept, names, *args):
    r = dict(zip(names, args))
    meta = r["meta"]
    step = pl.program_id(0)
    last = pl.num_programs(0) - 1
    layers, rows, patches, depth, m = sz.layers, sz.rows, sz.patches, sz.depth, sz.m
    alone = kept != sz.own
    whole = patches // 16 * 16
    pair = 2 * rows
    blocks = [slice(i, min(i + pair, m)) for i in range(0, m, pair)]
    lane = lax.broadcasted_iota(jnp.int32, (1, depth), 1)
    columns = pl.ds(pl.multiple_of(meta[1 if alone else 2] * kept, 128), kept)
    mine = pl.ds(pl.multiple_of(meta[0] * sz.own, 128), sz.own)
    theirs = pl.ds(pl.multiple_of(meta[3] * sz.own, 128), sz.own)
    x, grad, gw = r["x"], r["grad"], r["gw"]

    group = pl.ds(pl.multiple_of(first_group(alone, meta) * GROUP, GROUP), GROUP)
    buffers = {"tok": r["tokb"], "cot": r["cotb"]}

    cut = patches // 2
    results = (("out", "tok", 0, patches), ("tgrad", "cot", 0, cut), ("tgrad", "cot", cut, patches))
    spots = sent_spots(sz)

    def deliver(i):
        name, source, start, stop = results[i]
        if alone:
            place = r[f"sent{spots[i][0]}"].at[spots[i][1] : spots[i][2]]
        else:
            place = r[name].at[start:stop, group, :]
        return pltpu.make_async_copy(buffers[source].at[start:stop], place, r["moved"].at[i])

    def bring(i):
        name, _, start, stop = results[i]
        place = r["pass_" + name].at[start:stop]
        source = r[f"own{spots[i][0]}"].at[spots[i][1] : spots[i][2]]
        return pltpu.make_async_copy(source, place, r["passed"].at[i])

    def pass_on(i):
        name, _, start, stop = results[i]
        at = pl.ds(pl.multiple_of(meta[0] * GROUP, GROUP), GROUP)
        source, place = r["pass_" + name].at[start:stop], r[name].at[start:stop, at, :]
        return pltpu.make_async_copy(source, place, r["passed"].at[i])

    def to_staging(name):
        staged = r[name + "f"]
        for c in range(sz.width // 128):
            part = r[name][:, :, c * 128 : (c + 1) * 128].astype(F32)
            staged[c, : patches * GROUP, :] = part.reshape(patches * GROUP, 128)
            staged[c, patches * GROUP :, :] = jnp.zeros(((rows - patches + 1) * GROUP, 128), F32)

    def from_staging(name):
        for c in range(sz.width // 128):
            v = r[name + "f"][c, : patches * GROUP, :].reshape(patches, GROUP, 128)
            buffers[name][:, :, c * 128 : (c + 1) * 128] = v.astype(BF)

    @pl.when(step == 0)
    def _():
        if sz.blocks:
            for l in range(layers):
                for i in range(2):
                    for half in range(2):
                        src = r[f"w{i}part{half}_{l}"]
                        n_part = src.shape[0]
                        for k in range(n_part):
                            at = meta[4 + l * sz.n_dp + half * n_part + k] * sz.shard
                            at = pl.ds(pl.multiple_of(at, 16), sz.shard)
                            pltpu.make_async_copy(
                                src.at[k], r["w"].at[i, l, at], r["arrive"].at[i, l]
                            ).start()
        if not alone:
            pltpu.make_async_copy(r["carry"], gw, r["carried"]).start()
            for i in range(3):
                bring(i).start()
        for name in ("gwc", "gsum", "gb1") + (("gw",) if alone else ()):
            r[name][...] = jnp.zeros_like(r[name])
        r["keep"][...] = jnp.zeros_like(r["keep"])
        first_image = first_group(alone, meta) * GROUP
        for g in range(GROUP):
            r["keep"][g, :, :patches] = r["masks"][pl.ds(first_image + g, 1), :].astype(F32)
        wc = r["wc"]
        wc[...] = jnp.zeros_like(wc)
        r["bias"][...] = jnp.zeros_like(r["bias"])
        for l in range(layers):
            r["bias"][:, :patches] = jnp.broadcast_to(r["cb"][l : l + 1, :], (128, patches))
            column = r["bias"][...].T[:rows, : depth - 128]
            high = column.astype(BF)
            low = (column - high.astype(F32)).astype(BF)
            wc[l, :patches, :patches] = r["cw"][l]
            at = lane[:, 128:]
            extra = jnp.where(at == patches, high, jnp.where(at == patches + 1, low, 0.0))
            wc[l, :, 128:] = wc[l, :, 128:] + extra.astype(BF)
        to_staging("tok")
        to_staging("cot")
        for l in range(layers):
            r["b1s"][l] = r["b1"][l : l + 1, :]
            r["b2s"][l] = r["b2"][l : l + 1, :]

    def weight_ready(i, l):
        if sz.blocks:

            @pl.when(step == 0)
            def _():
                ref = r["w"].at[i, l]
                pltpu.make_async_copy(ref, ref, r["arrive"].at[i, l]).wait()

    def weight(i, l):
        return r["w"][i, l]

    def keep_of(g):
        return r["keep"][step * STEP + g]

    def row(name, l, k):
        return r[name][l, k : k + 1, :]

    def image(g):
        return slice(g * rows, (g + 1) * rows)

    def add(l, kind, v):
        r["gsum"][l, kind] += jnp.sum(v.reshape(v.shape[0] // 8, 8, v.shape[1]), axis=0)

    def unstage(name, g):
        at = pl.ds(step * STEP + g, rows, stride=GROUP)
        return jnp.concatenate([r[name][c, at, :] for c in range(sz.width // 128)], axis=1)

    def stage(name, g, v):
        at = pl.ds(step * STEP + g, rows, stride=GROUP)
        for c in range(sz.width // 128):
            r[name][c, at, :] = v[:, c * 128 : (c + 1) * 128]

    for g in range(STEP):
        x[0, image(g), :] = unstage("tokf", g)
    share = STEP // layers

    def rows_of(g):
        return pl.ds(pl.multiple_of(g * rows, 8), rows)

    def forward(l, _):
        for g in range(share):
            grad[rows_of(l * share + g), :] = unstage("cotf", l * share + g)
        mid, mixed, crossed = r["mid"], r["mixed"], r["crossed"]
        for g in range(STEP):
            x_in = x[l, image(g), :]
            v = x_in * row("scale", l, 0) + row("shift", l, 0)
            mixed[l, g, :whole, :] = v[:whole].astype(BF)
            left = lax.broadcasted_iota(jnp.int32, (rows - whole, 1), 0) + whole
            tail = jnp.where(left < patches, v[whole:], 1.0)
            if depth > rows:
                tail = jnp.concatenate([tail, jnp.ones((depth - rows, sz.width), F32)], axis=0)
            mixed[l, g, whole:, :] = tail.astype(BF)
            wk = r["wc"][l] * jnp.where(lane < patches, keep_of(g), 1.0).astype(BF)
            c = dot(wk, mixed[l, g], NN)
            crossed[l, g, :rows, :] = c.astype(BF)
            mid[l, image(g), :] = x_in + row("ls", l, 0) * c
        for at in blocks:
            v = mid[l, at, :] * row("scale", l, 1) + row("shift", l, 1)
            r["normed"][l, at, :] = v.astype(BF)
        weight_ready(0, l)
        for at in blocks:
            h = dot(r["normed"][l, at, :], weight(0, l), NN) + r["b1s"][l]
            phi = 0.5 + 0.5 * lax.erf(h * SQRT_HALF)
            r["act"][l, at, :] = (h * phi).astype(BF)
            r["h"][l, at, :] = h.astype(BF)
            r["phi"][l, at, :] = phi.astype(BF)
        weight_ready(1, l)
        for at in blocks:
            branch = dot(r["act"][l, at, :], weight(1, l), NT) + r["b2s"][l]
            r["branch"][l, at, :] = branch.astype(BF)
            x[l + 1, at, :] = mid[l, at, :] + row("ls", l, 1) * branch
    lax.fori_loop(0, layers, forward, None)
    @pl.when(step == 0)
    def _():
        if not alone:
            pltpu.make_async_copy(r["carry"], gw, r["carried"]).wait()

    @pl.when(step == last)
    def _():
        if not alone:
            for i in range(3):
                bring(i).wait()
                pass_on(i).start()

    def backward(back, _):
        l = layers - 1 - back
        for g in range(share):
            stage("tokf", back * share + g, x[layers, rows_of(back * share + g), :])
        for at in blocks:
            g_out = grad[at, :]
            add(l, LS1, g_out * r["branch"][l, at, :].astype(F32))
            bg = row("ls", l, 1) * g_out
            add(l, B2, bg)
            r["bg"][at, :] = bg.astype(BF)
        for at in blocks:
            act_grad = dot(r["bg"][at, :], weight(1, l), NN)
            h = r["h"][l, at, :]
            density = jnp.exp2(h * h * BF(HALF_LOG2E)) * BF(PDF_SCALE)
            r["pg"][at, :] = act_grad.astype(BF) * (r["phi"][l, at, :] + h * density)
        pg = r["pg"][:, columns]
        r["gb1"][l] += jnp.sum(pg.astype(F32).reshape(m // 8, 8, kept), axis=0)
        gw[0, l] += dot(r["normed"][l], pg, TN)
        gw[1, l] += dot(r["bg"][...], r["act"][l, :, columns], TN)
        for at in blocks:
            normed_grad = dot(r["pg"][at, :], weight(0, l), NT)
            add(l, S1, normed_grad * r["mid"][l, at, :])
            add(l, T1, normed_grad)
            grad[at, :] += row("scale", l, 1) * normed_grad
        for g in range(STEP):
            at = image(g)
            keep = keep_of(g)
            mg = grad[at, :]
            add(l, LS0, mg * r["crossed"][l, g, :rows, :].astype(F32))
            cg = (row("ls", l, 0) * mg).astype(BF)
            r["gwc"][l] += dot(cg, r["mixed"][l, g], NT) * jnp.where(lane < patches, keep, 1.0)
            wk = r["wc"][l] * jnp.where(lane < patches, keep, 0.0).astype(BF)
            mixed_grad = dot(wk, cg, TN)[:rows]
            add(l, S0, mixed_grad * x[l, at, :])
            add(l, T0, mixed_grad)
            grad[at, :] = mg + row("scale", l, 0) * mixed_grad
    lax.fori_loop(0, layers, backward, None)
    for g in range(STEP):
        stage("cotf", g, grad[image(g), :])

    @pl.when(step == last)
    def _():
        def write_small(ref, wanted):
            for l in range(layers):
                sums = [jnp.sum(r["gsum"][l, k], axis=0, keepdims=True) for k in range(B1)]
                sums.append(jnp.sum(r["gb1"][l, :, wanted], axis=0, keepdims=True))
                table = jnp.concatenate(sums, axis=0)
                low = r["gwc"][l, :, :128]
                high = jnp.pad(r["gwc"][l, :, 128:], ((0, 0), (0, 256 - depth)))
                a, b = sz.tall, 2 * sz.tall - rows
                last_part = jnp.pad(high[b:], ((0, 3 * a - 2 * rows), (0, 0)))
                middle = jnp.concatenate([low[a:], high[:b]], axis=0)
                wide = jnp.concatenate([low[:a], middle, last_part], axis=1)
                full = jnp.concatenate([wide, table], axis=0)
                if ref.shape[1] == 8:
                    n = sz.small // 8
                    full = full.reshape(n, 8, sz.width)
                    ref[l * n : (l + 1) * n] = full.astype(BF)
                else:
                    ref[l] = full.astype(BF)

        from_staging("tok")
        deliver(0).start()
        from_staging("cot")
        deliver(1).start()
        deliver(2).start()

        if alone:
            write_small(r["small"], mine)
            write_small(r["sends"], theirs)
            tail = spots[1][2]
            pltpu.make_async_copy(r["sends"], r["sent0"].at[tail:], r["moved"].at[3]).start()
            for i in range(2):
                for l in range(layers):
                    r["own"][i, l] = gw[i, l, :, mine]
                    for k in range(sz.n_dp if sz.blocks else 1):
                        size = sz.shard if sz.blocks else sz.width
                        place = slice(k * size, (k + 1) * size)
                        r["blocks"][k, i, l] = gw[i, l, place, theirs].astype(BF)
        else:
            write_small(r["small"], slice(None))
            for i in range(2):
                if sz.blocks:
                    n = sz.n_dp // 2
                    for k in range(sz.n_dp):
                        at = meta[4 + (2 + i) * sz.n_dp + k] * sz.shard
                        at = pl.ds(pl.multiple_of(at, 16), sz.shard)
                        ref = r[f"stay{i}"] if k < n else r[f"leave{i}"]
                        for l in range(layers):
                            to = (k % n) * sz.slot + l * sz.shard
                            ref[to : to + sz.shard, :] = gw[i, l, at, :].astype(BF)
                else:
                    for l in range(layers):
                        r[f"stay{i}"][l * sz.width : (l + 1) * sz.width, :] = gw[i, l].astype(BF)
            for i in range(3):
                pass_on(i).wait()
        for i in range(3):
            deliver(i).wait()
        if alone:
            tail = spots[1][2]
            pltpu.make_async_copy(r["sends"], r["sent0"].at[tail:], r["moved"].at[3]).wait()


def run(sz, alone, meta, common, weights, first=None):
    steps = GROUP // STEP
    w, m, layers = sz.width, sz.m, sz.layers
    kept = 2 * sz.own if alone else sz.own
    vmem = pl.BlockSpec(memory_space=pltpu.VMEM)
    anywhere = pl.BlockSpec(memory_space=pl.ANY)
    images = (sz.patches, GROUP, w)

    group_spec = pl.BlockSpec(
        images, lambda i, meta: (0, first_group(alone, meta), 0), pipeline_mode=pl.Buffered(1)
    )

    def fixed_spec(block):
        return pl.BlockSpec(
            block, lambda i, meta: (0,) * len(block), pipeline_mode=pl.Buffered(1)
        )

    ins = [
        ("tok", common["tok"], group_spec),
        ("cot", common["cot"], group_spec),
    ]
    for name in ("masks", "scale", "shift", "ls", "cw", "cb", "b1", "b2"):
        ins.append((name, common[name], vmem))
    scratch = []
    if sz.blocks:
        for l in range(layers):
            for i in range(2):
                for half in range(2):
                    ins.append((f"w{i}part{half}_{l}", weights[l][i][half], anywhere))
        scratch.append(("w", pltpu.VMEM((2, layers, w, sz.hidden), BF)))
        scratch.append(("arrive", pltpu.SemaphoreType.DMA((2, layers))))
    else:
        ins.append(("w", weights, vmem))
    if not alone:
        ins.append(("carry", first["own"], anywhere))
        for i in range(2):
            ins.append((f"own{i}", first[f"sent{i}"], anywhere))
        scratch.append(("passed", pltpu.SemaphoreType.DMA((3,))))
        scratch.append(("pass_out", pltpu.VMEM(images, BF)))
        scratch.append(("pass_tgrad", pltpu.VMEM(images, BF)))
        scratch.append(("carried", pltpu.SemaphoreType.DMA))

    if alone:
        spots, packed = sent_spots(sz), layers * sz.small // GROUP
        parts = (("sent0", spots[1][2] + packed), ("sent1", spots[2][2]))
        outs = [(name, (n, GROUP, w), BF, anywhere) for name, n in parts]
        scratch.append(("sends", pltpu.VMEM((packed, GROUP, w), BF)))
    else:
        outs = [(name, (sz.patches, sz.count, w), BF, anywhere) for name in ("out", "tgrad")]
    small = (layers, sz.small, w)
    block = (layers, sz.shard, sz.own) if sz.blocks else (layers, w, sz.own)
    n_blocks = sz.n_dp if sz.blocks else 1
    outs.append(("small", small, BF, fixed_spec(small)))
    if not alone:
        part = ((n_blocks + 1) // 2 * block[0] * block[1], sz.own)
        for name in ("stay0", "stay1") + (("leave0", "leave1") if sz.blocks else ()):
            outs.append((name, part, BF, fixed_spec(part)))
    else:
        outs.append(("blocks", (n_blocks, 2) + block, BF, fixed_spec((n_blocks, 2) + block)))
        own = (2, layers, w, sz.own)
        outs.append(("own", own, F32, fixed_spec(own)))
    for name, shape, dtype in (
        ("x", (layers + 1, m, w), F32),
        ("mid", (layers, m, w), F32),
        ("crossed", (layers, STEP, sz.depth, w), BF),
        ("mixed", (layers, STEP, sz.depth, w), BF),
        ("normed", (layers, m, w), BF),
        ("h", (layers, m, sz.hidden), BF),
        ("phi", (layers, m, sz.hidden), BF),
        ("act", (layers, m, sz.hidden), BF),
        ("branch", (layers, m, w), BF),
        ("grad", (m, w), F32),
        ("bg", (m, w), BF),
        ("pg", (m, sz.hidden), BF),
        ("gw", (2, layers, w, kept), F32),
        ("gwc", (layers, sz.rows, sz.depth), F32),
        ("gsum", (layers, B1, 8, w), F32),
        ("gb1", (layers, 8, kept), F32),
        ("keep", (GROUP, 1, sz.depth), F32),
        ("wc", (layers, sz.rows, sz.depth), BF),
        ("bias", (128, 256), F32),
        ("b1s", (layers, 1, sz.hidden), F32),
        ("b2s", (layers, 1, w), F32),
        ("tokb", images, BF),
        ("cotb", images, BF),
        ("tokf", (w // 128, GROUP * (sz.rows + 1), 128), F32),
        ("cotf", (w // 128, GROUP * (sz.rows + 1), 128), F32),
    ):
        scratch.append((name, pltpu.VMEM(shape, dtype)))
    scratch.append(("moved", pltpu.SemaphoreType.DMA((4,))))
    names = ("meta",) + tuple(e[0] for e in ins + outs + scratch)
    flops = steps * m * 24 * w * sz.hidden
    results = pl.pallas_call(
        functools.partial(kernel_body, sz, kept, names),
        grid_spec=pltpu.PrefetchScalarGridSpec(
            num_scalar_prefetch=1,
            grid=(steps,),
            in_specs=[e[2] for e in ins],
            out_specs=[e[3] for e in outs],
            scratch_shapes=[e[1] for e in scratch],
        ),
        out_shape=[jax.ShapeDtypeStruct(e[1], e[2]) for e in outs],
        compiler_params=pltpu.CompilerParams(vmem_limit_bytes=60 * 2**20),
        cost_estimate=pl.CostEstimate(flops=flops, bytes_accessed=flops // 400, transcendentals=0),
    )(meta, *[e[1] for e in ins])
    return {e[0]: value for e, value in zip(outs, results)}


def swap(x, axis, k):
    n = lax.axis_size(axis)
    return lax.ppermute(x, axis, [(i, i ^ k) for i in range(n)])


def powers(n):
    return [2**k for k in range(1, n.bit_length() - 1)]


def gather_columns(sz, both, later, hid):
    parts = [both] + [swap(both, "hid", k) for k in range(1, sz.n_hid)]
    if later is not None:
        parts[1:3], later = lax.optimization_barrier((parts[1:3], later))
    columns = []
    for j in range(sz.n_hid):
        v = parts[j]
        for h in range(1, sz.n_hid):
            v = jnp.where(hid == h, parts[j ^ h], v)
        columns.append(v)
    return jnp.concatenate(columns, axis=2), later


def gather_rows(sz, full):
    got = [full[i][None] for i in range(2)]
    bits = powers(sz.n_dp)
    for step in range(len(bits)):
        moved = [swap(got[0], "dp", bits[step]), swap(got[1], "dp", bits[-1 - step])]
        got = [jnp.concatenate([g, v]) for g, v in zip(got, moved)]
    return got


def gather_orders(n_dp):
    bits, orders = powers(n_dp), []
    for seq in (bits, bits[::-1]):
        order = [0]
        for b in seq:
            order += [o ^ b for o in order]
        orders.append(order + [o ^ 1 for o in order])
    return orders


def exchange_orders(n_dp):
    bits = powers(n_dp)
    result = []
    for seq in ([1] + bits, [1] + bits[::-1]):
        order = [0]
        for b in reversed(seq):
            order = order + [o ^ b for o in order]
        result.append((seq, order))
    return result


def place_body(sz, meta, sent0, sent1, _, __, out, tgrad, pass0, pass1, pass2, moved):
    place = pl.ds(pl.multiple_of(meta[3] * GROUP, GROUP), GROUP)
    cut = sz.patches // 2
    to = (out.at[:, place, :], tgrad.at[:cut, place, :], tgrad.at[cut:, place, :])
    brought, copies = [], []
    for i, buffer in enumerate((pass0, pass1, pass2)):
        which, start, stop = sent_spots(sz)[i]
        source = (sent0, sent1)[which].at[start:stop]
        brought.append(pltpu.make_async_copy(source, buffer, moved.at[i]))
        copies.append(pltpu.make_async_copy(buffer, to[i], moved.at[i]))
        brought[i].start()
    for i in range(3):
        brought[i].wait()
        copies[i].start()
    for c in copies:
        c.wait()


def place_images(sz, meta, sent, out, tgrad):
    anywhere = pl.BlockSpec(memory_space=pl.ANY)
    whole = jax.ShapeDtypeStruct(out.shape, BF)
    buffers = [(stop - start, GROUP, sz.width) for _, start, stop in sent_spots(sz)]
    return pl.pallas_call(
        functools.partial(place_body, sz),
        grid_spec=pltpu.PrefetchScalarGridSpec(
            num_scalar_prefetch=1,
            grid=(),
            in_specs=[anywhere] * 4,
            out_specs=[anywhere] * 2,
            scratch_shapes=[pltpu.VMEM(shape, BF) for shape in buffers]
            + [pltpu.SemaphoreType.DMA((3,))],
        ),
        out_shape=[whole, whole],
        input_output_aliases={3: 0, 4: 1},
        compiler_params=pltpu.CompilerParams(vmem_limit_bytes=16 * 2**20),
        cost_estimate=pl.CostEstimate(
            flops=0, bytes_accessed=8 * out.size // 3, transcendentals=0
        ),
    )(meta, *sent, out, tgrad)


def phase_body(sz, n, *refs):
    stays, gots, smalls, got_smalls = refs[:2], refs[2:4], refs[4:6], refs[6:8]
    keeps, pays = refs[8:10], refs[10:12]
    cut = n // 2 * sz.slot
    for i in range(2):
        total = stays[i][: n * sz.slot].astype(F32) + gots[i][: n * sz.slot].astype(F32)
        keeps[i][...] = total[:cut]
        pays[i][: n * sz.slot - cut] = total[cut:].astype(BF)
        own = smalls[i][smalls[i].shape[0] - sz.small :].astype(F32)
        other = got_smalls[i][got_smalls[i].shape[0] - sz.small :].astype(F32)
        pays[i][n * sz.slot - cut :] = (own + other).astype(BF)


def first_phase_body(sz, n, *refs):
    small, got_small, parts, total = refs[4], refs[5], refs[6], refs[11]
    smalls, got_smalls = ([v.at[i] for i in range(2)] for v in (small, got_small))
    phase_body(sz, n, *refs[:4], *smalls, *got_smalls, *refs[7:11])
    for i in range(2):
        v = parts[0, i].astype(F32)
        for k in range(1, sz.n_dp):
            v = v + parts[k, i].astype(F32)
        total[i] = v.astype(BF).reshape(sz.slot, sz.own)


def first_phase(sz, n, stays, gots, small, got_small, parts):
    if sz.blocks:
        cut = n // 2 * sz.slot
        keep = jax.ShapeDtypeStruct((cut, sz.own), F32)
        pay = jax.ShapeDtypeStruct((n * sz.slot - cut + sz.small, sz.own), BF)
        total = jax.ShapeDtypeStruct((2, sz.slot, sz.own), BF)
        out = pl.pallas_call(
            functools.partial(first_phase_body, sz, n),
            in_specs=[pl.BlockSpec(memory_space=pltpu.VMEM)] * 7,
            out_specs=[pl.BlockSpec(memory_space=pltpu.VMEM)] * 5,
            out_shape=[keep, keep, pay, pay, total],
            compiler_params=pltpu.CompilerParams(vmem_limit_bytes=32 * 2**20),
        )(*stays, *gots, small, got_small, parts)
        return out[:2], out[2:4], out[4]
    keeps, pays = phase(sz, n, stays, gots, small, got_small)
    return keeps, pays, parts.astype(F32).sum(axis=0).astype(BF).reshape(2, sz.slot, sz.own)


def phase(sz, n, stays, gots, smalls, got_smalls):
    if sz.blocks:
        cut = n // 2 * sz.slot
        keep = jax.ShapeDtypeStruct((cut, sz.own), F32)
        pay = jax.ShapeDtypeStruct((n * sz.slot - cut + sz.small, sz.own), BF)
        out = pl.pallas_call(
            functools.partial(phase_body, sz, n),
            in_specs=[pl.BlockSpec(memory_space=pltpu.VMEM)] * 8,
            out_specs=[pl.BlockSpec(memory_space=pltpu.VMEM)] * 4,
            out_shape=[keep, keep, pay, pay],
            compiler_params=pltpu.CompilerParams(vmem_limit_bytes=32 * 2**20),
        )(*stays, *gots, *smalls, *got_smalls)
        return out[:2], out[2:]
    keeps, pays = [], []
    for i in range(2):
        total = stays[i].astype(F32) + gots[i][: n * sz.slot].astype(F32)
        cut = n // 2 * sz.slot
        own, other = smalls[i][-sz.small :].astype(F32), got_smalls[i][-sz.small :].astype(F32)
        keeps.append(total[:cut])
        pays.append(jnp.concatenate([total[cut:], own + other]).astype(BF))
    return keeps, pays


def finish_body(sz, *refs):
    keeps, pays, gots, theirs = refs[0:2], refs[2:4], refs[4:6], refs[6]
    (scale, shift, ls, gwc, gb, w1, b1, w2, b2) = refs[7:]
    for i, ref in enumerate((w1, w2)):
        total = keeps[i][...] + gots[i][: keeps[i].shape[0]].astype(F32)
        ref[...] = total + theirs[i].astype(F32)
    for l in range(2):
        at = pays[l].shape[0] - sz.small
        total = pays[l][at:].astype(F32) + gots[l][at:].astype(F32)
        a, b = sz.tall, 2 * sz.tall - sz.rows
        low = jnp.concatenate([total[:a, :128], total[: sz.rows - a, 128:256]], axis=0)
        high = jnp.concatenate([total[sz.rows - a : a, 128:256], total[: sz.rows - b, 256:]], axis=0)
        gwc[:, l, :] = jnp.concatenate([low, high], axis=1)[: sz.patches, : sz.patches]
        lane = sz.patches - 128
        gb[l : l + 1, :] = high.T[lane : lane + 1, : sz.patches]
        table = total[a : a + 8]
        for ref, kinds in ((scale, (S0, S1)), (shift, (T0, T1)), (ls, (LS0, LS1))):
            for k, kind in enumerate(kinds):
                ref[l, k : k + 1, :] = table[kind : kind + 1]
        b1[l : l + 1, :] = table[B1 : B1 + 1]
        b2[l : l + 1, :] = table[B2 : B2 + 1]


def finish(sz, keeps, pays, gots, theirs):
    vmem = pl.BlockSpec(memory_space=pltpu.VMEM)
    layers, w, p = sz.layers, sz.width, sz.patches
    vec, rows = (layers, 2, w), (sz.slot, sz.own)
    if sz.slot % 16:
        gap = ((0, round_up(sz.slot, 16) - sz.slot), (0, 0))
        pays, gots = (
            [jnp.concatenate([jnp.pad(v[: sz.slot], gap), v[sz.slot :]]) for v in vs]
            for vs in (pays, gots)
        )
        keeps = [jnp.pad(v, gap) for v in keeps]
        theirs = jnp.pad(theirs, ((0, 0),) + gap)
        rows = (round_up(sz.slot, 16), sz.own)
    shapes = [vec, vec, vec, (p, layers, p), (layers, p), rows, (layers, sz.own), rows, (layers, w)]
    result = list(
        pl.pallas_call(
            functools.partial(finish_body, sz),
            in_specs=[vmem] * 7,
            out_specs=[vmem] * 9,
            out_shape=[jax.ShapeDtypeStruct(s, F32) for s in shapes],
            compiler_params=pltpu.CompilerParams(vmem_limit_bytes=32 * 2**20),
        )(*keeps, *pays, *gots, theirs)
    )
    for i in (5, 7):
        result[i] = result[i][: sz.slot].reshape(layers, sz.shard, sz.own)
    return result


def on_device(
    tokens,
    masks,
    cotangent,
    aff_scale,
    aff_shift,
    layer_scale,
    crosspatch_weight,
    cross_bias,
    fc1_weight,
    fc1_bias,
    fc2_weight,
    fc2_bias,
):
    n_dp, n_hid = lax.axis_size("dp"), lax.axis_size("hid")
    sz = Sizes(tokens, fc1_weight, n_dp, n_hid)
    layers, patches = sz.layers, sz.patches
    me, hid = lax.axis_index("dp"), lax.axis_index("hid")
    half = hid % 2

    orders, exchanges = gather_orders(n_dp), exchange_orders(n_dp)
    places = [half, hid // 2, hid, 1 - half] + [me ^ k for k in orders[0] + orders[1]]
    places += [me ^ k for k in exchanges[0][1] + exchanges[1][1]]
    meta = jnp.stack(places).astype(jnp.int32)

    weights = []
    gathered, later, chip = [], fc2_weight, hid
    for i in range(2):
        full, later = gather_columns(sz, later if i else fc1_weight, None if i else later, chip)
        full, chip = lax.optimization_barrier((full, chip))
        got = gather_rows(sz, full)
        if i == 0:
            got, meta = lax.optimization_barrier((got, meta))
        gathered.append((got, [swap(g, "dp", 1) for g in got]))
    for l in range(layers):
        got, other = ([gathered[i][part][l] for i in range(2)] for part in range(2))
        if sz.blocks:
            weights.append([(got[i], other[i]) for i in range(2)])
        else:
            ready = []
            for i in range(2):
                w = jnp.concatenate([got[i], other[i]])
                at = jnp.zeros(n_dp, jnp.int32).at[jnp.array(orders[l])].set(jnp.arange(n_dp))
                w = w[at[jnp.arange(n_dp) ^ me]]
                ready.append(w.reshape(sz.width, sz.hidden))
            weights.append(jnp.stack(ready))
    if not sz.blocks:
        weights = jnp.stack(weights, axis=1)

    common = {
        "tok": tokens.transpose(1, 0, 2),
        "cot": cotangent.transpose(1, 0, 2),
        "masks": masks,
        "scale": aff_scale,
        "shift": aff_shift,
        "ls": layer_scale,
        "cw": crosspatch_weight,
        "cb": cross_bias,
        "b1": fc1_bias,
        "b2": fc2_bias,
    }
    first = run(sz, True, meta, common, weights)
    sent = [swap(first[f"sent{i}"], "hid", 1) for i in range(2)]

    theirs = first["blocks"]
    if not sz.blocks:
        theirs = theirs.reshape(2, layers, n_dp, sz.shard, sz.own)
        theirs = jnp.moveaxis(theirs, 2, 0)
    theirs = lax.all_to_all(theirs, "dp", split_axis=0, concat_axis=0, tiled=True)

    rest = run(sz, False, meta, common, weights, first)
    stays = [rest[f"stay{i}"] for i in range(2)]
    if sz.blocks:
        leaves = [rest[f"leave{i}"] for i in range(2)]
    else:
        whole = [g.reshape(layers, n_dp, sz.shard, sz.own) for g in stays]
        whole = [jnp.moveaxis(g, 1, 0)[jnp.array(e[1]) ^ me] for g, e in zip(whole, exchanges)]
        whole = [g.reshape(2, -1, sz.own) for g in whole]
        stays, leaves = [g[0] for g in whole], [g[1] for g in whole]
    leaves, theirs, sent[0] = lax.optimization_barrier((leaves, theirs, sent[0]))
    small = sent[0][sent_spots(sz)[1][2] :].reshape(layers, sz.small, sz.width)
    small = first["small"].astype(F32) + small.astype(F32)
    small = (small + rest["small"].astype(F32)).astype(BF)
    got_small = swap(small, "dp", 1)
    gots = [swap(v, "dp", 1) for v in leaves]
    n = n_dp // 2
    keeps, pays, theirs = first_phase(sz, n, stays, gots, small, got_small, theirs)
    theirs = swap(theirs, "hid", 1)
    for k in range(1, len(exchanges[0][0]) - 1):
        n //= 2
        gots = [swap(pays[i], "dp", exchanges[i][0][k]) for i in range(2)]
        keeps, pays = phase(sz, n, keeps, gots, pays, gots)
    gots = [swap(pays[i], "dp", exchanges[i][0][-1]) for i in range(2)]
    out, tgrad = place_images(sz, meta, sent, rest["out"], rest["tgrad"])
    scale, shift, ls, gwc, gb, w1, b1, w2, b2 = finish(sz, keeps, pays, gots, theirs)
    return (
        out.transpose(1, 0, 2),
        tgrad.transpose(1, 0, 2),
        scale,
        shift,
        ls,
        gwc.transpose(1, 0, 2),
        gb,
        w1,
        b1,
        w2,
        b2,
    )


def solution(mesh):
    return jax.shard_map(
        on_device,
        mesh=mesh,
        in_specs=(
            P("dp", None, None),
            P("dp", None),
            P("dp", None, None),
            P(),
            P(),
            P(),
            P(),
            P(),
            P(None, "dp", "hid"),
            P(),
            P(None, "dp", "hid"),
            P(),
        ),
        out_specs=(
            P("dp", None, None),
            P("dp", None, None),
            P(),
            P(),
            P(),
            P(),
            P(),
            P(None, "dp", "hid"),
            P(None, "hid"),
            P(None, "dp", "hid"),
            P(),
        ),
        check_vma=False,
    )
```
